32 devices in a mesh: parts: 2 (over x), row: 16 (over z, y, core).
Axes of the slice: x: 2, y: 2, z: 4, core: 2. Of those that a mesh axis runs over, the one named last changes fastest.
Arguments:
- latent: bfloat16 [64, 256, 512], P(('parts', 'row')), parts along dimension 0, may hold values from -6 to 6
- conv_first: bfloat16 [3, 3, 512, 512], P(None, None, 'row'), may hold values from -0.09375 to 0.09375
- conv_second: bfloat16 [3, 3, 512, 512], P(None, None, 'row'), may hold values from -0.09375 to 0.09375
- w_query: bfloat16 [512, 512], replicated
- w_key: bfloat16 [512, 512], replicated
- w_value: bfloat16 [512, 512], replicated, may hold values from -0.25 to 0.25
- w_out: bfloat16 [512, 512], replicated, may hold values from -0.25 to 0.25
- w_in: bfloat16 [512, 2048], replicated, may hold values from -0.25 to 0.25
- w_down: bfloat16 [2048, 512], replicated, may hold values from -0.125 to 0.125
- conv_up: bfloat16 [3, 3, 512, 512], P(None, None, 'row'), may hold values from -0.09375 to 0.09375
Outputs:
- latent_out: bfloat16 [64, 256, 512], P(('parts', 'row')), parts along dimension 0
- upsampled: bfloat16 [64, 256, 512], P('parts', 'row'), parts along dimension 0
The draws below stay inside these ranges and needn't reach their ends.
There are 2 independent parts, one for each index of `parts`. The reference program is written for one: setup_inputs(seed, part) draws one part's arguments, and reference() takes and returns one part's arrays. A program takes and returns all parts, laid end to end along the dimension named above; an argument that names none is the same for every part. Nothing has to cross between parts.
All inputs are finite; a program needn't handle non-finite values.
Results may differ from the reference program's by a relative error of at most 0.015.
Values may be sent and summed in bfloat16 or wider, within the bound.
No kernel may reach another device: no remote copies, remote signals or barrier semaphores. Data moves between devices by JAX's collectives and lax.ppermute only.
A program may use at most 128 MiB of HBM per device.

```python
import math
import jax
import jax.numpy as jnp
from jax import lax

C = 512
HEADS = 8
HD = 64
FF = 2048
GRID = 16
W = 256
H = 32


def common_matrix(key):
    return jax.random.normal(jax.random.fold_in(key, 7), (C, C), jnp.float32)


def draw_w_query(key, part):
    common = common_matrix(key)
    return (common * (1.0 / math.sqrt(C))).astype(jnp.bfloat16)


def draw_w_key(key, part):
    private = jax.random.normal(jax.random.fold_in(key, 8), (C, C), jnp.float32)
    return (private * (1.0 / math.sqrt(C))).astype(jnp.bfloat16)


def level_of(key, extent, cuts, smallest, high):
    def one(position, parts):
        steps = jax.random.uniform(jax.random.fold_in(jax.random.fold_in(key, 6), position), (parts,), jnp.float32, smallest / len(cuts), high / len(cuts))
        return jnp.repeat(jnp.exp(steps), extent[position] // parts).reshape((-1,) + (1,) * (len(extent) - position - 1))

    factor_of = one(*cuts[0])
    for cut in cuts[1:]:
        factor_of = factor_of * one(*cut)
    return factor_of


def centred(rng, extent, spread, bound, cuts=(), kind=jnp.bfloat16):
    loudness = level_of(rng, extent, cuts, -0.22, 0.18) if cuts else 1.0
    drawn = jax.random.normal(rng, extent, jnp.float32) * spread * loudness
    return jnp.minimum(jnp.maximum(drawn, -bound), bound).astype(kind)


def setup_inputs(seed: int = 0, part: int = 0) -> dict:
    keys = jax.random.split(jax.random.key(seed), 11)
    part_keys = jax.random.split(jax.random.fold_in(keys[10], part), 11)
    return {
        "latent": centred(part_keys[0], (H, W, C), 1.0, 6.0, ((0, 16),)),
        "conv_first": centred(keys[1], (3, 3, C, C), (9 * C) ** -0.5, 0.09375, ((2, 16),)),
        "conv_second": centred(keys[2], (3, 3, C, C), (9 * C) ** -0.5, 0.09375, ((2, 16),)),
        "w_query": draw_w_query(jax.random.fold_in(keys[10], 71), part),
        "w_key": draw_w_key(jax.random.fold_in(keys[10], 71), part),
        "w_value": centred(keys[5], (C, C), C ** -0.5, 0.25),
        "w_out": centred(keys[6], (C, C), C ** -0.5, 0.25),
        "w_in": centred(keys[7], (C, FF), C ** -0.5, 0.25),
        "w_down": centred(keys[8], (FF, C), FF ** -0.5, 0.125),
        "conv_up": centred(keys[9], (3, 3, C, C), (9 * C) ** -0.5, 0.09375, ((2, 16),)),
    }


def rms_round(values):
    meansq = lax.optimization_barrier(jnp.mean(values * values, axis=-1, keepdims=True))
    return (values * lax.rsqrt(meansq + 1e-06)).astype(jnp.bfloat16)

def convolve(field, kernel):
    height, breadth, channels = field.shape
    padded = jnp.pad(field, ((1, 1), (1, 1), (0, 0)))
    running = jnp.zeros((height * breadth, kernel.shape[3]), jnp.float32)
    for shift_row in range(3):
        for shift_col in range(3):
            window = padded[shift_row:shift_row + height, shift_col:shift_col + breadth].reshape(-1, channels)
            running = running + jnp.dot(window, kernel[shift_row, shift_col], preferred_element_type=jnp.float32)
    return running.reshape(height, breadth, kernel.shape[3])

def softmax_round(scores):
    highest = lax.optimization_barrier(jnp.max(scores, axis=-1, keepdims=True))
    lifted = jnp.exp(scores - highest)
    return (lifted / lax.optimization_barrier(jnp.sum(lifted, axis=-1, keepdims=True))).astype(jnp.bfloat16)

def reference(latent, conv_first, conv_second, w_query, w_key, w_value, w_out, w_in, w_down, conv_up):
    current = latent
    for kernel in (conv_first, conv_second):
        active = jax.nn.gelu(current.astype(jnp.float32)).astype(jnp.bfloat16)
        current = (current.astype(jnp.float32) + convolve(active, kernel)).astype(jnp.bfloat16)
    height, breadth, channels = current.shape
    normed = rms_round(current.astype(jnp.float32)).reshape(-1, channels)
    queries = jnp.dot(normed, w_query, preferred_element_type=jnp.float32).astype(jnp.bfloat16)
    keys_all = jnp.dot(normed, w_key, preferred_element_type=jnp.float32).astype(jnp.bfloat16)
    values_all = jnp.dot(normed, w_value, preferred_element_type=jnp.float32).astype(jnp.bfloat16)
    band_rows = height // GRID
    band_cols = breadth // GRID
    scale = HD ** (-0.5)

    def windows(tensor):
        return tensor.reshape(GRID, band_rows, GRID, band_cols, HEADS, HD).transpose(1, 0, 2, 3, 4, 5)

    def attend(blocks):
        query_block, key_block, value_block = blocks
        scores = jnp.einsum('abchd,efchd->chabef', query_block.astype(jnp.float32), key_block.astype(jnp.float32)) * scale
        scores = scores.reshape(band_cols, HEADS, GRID * GRID, GRID * GRID)
        probs = softmax_round(scores).reshape(band_cols, HEADS, GRID, GRID, GRID, GRID)
        output = jnp.einsum('chabef,efchd->abchd', probs.astype(jnp.float32), value_block.astype(jnp.float32))
        return output.astype(jnp.bfloat16)
    attended = lax.map(attend, (windows(queries), windows(keys_all), windows(values_all)))
    attended = attended.transpose(1, 0, 2, 3, 4, 5).reshape(-1, channels)
    projected = jnp.dot(attended, w_out, preferred_element_type=jnp.float32).reshape(height, breadth, channels)
    current = (current.astype(jnp.float32) + projected).astype(jnp.bfloat16)
    normed_two = rms_round(current.astype(jnp.float32)).reshape(-1, channels)
    hidden = jax.nn.gelu(jnp.dot(normed_two, w_in, preferred_element_type=jnp.float32)).astype(jnp.bfloat16)
    lowered = jnp.dot(hidden, w_down, preferred_element_type=jnp.float32).reshape(height, breadth, channels)
    latent_out = (current.astype(jnp.float32) + lowered).astype(jnp.bfloat16)
    central = latent_out[height // 4:3 * height // 4, breadth // 4:3 * breadth // 4]
    doubled = jnp.repeat(jnp.repeat(central, 2, axis=0), 2, axis=1)
    upsampled = convolve(doubled, conv_up).astype(jnp.bfloat16)
    return (latent_out, upsampled)
```

```python
import functools

import jax
import jax.numpy as jnp
from jax import lax
from jax.experimental import pallas as pl
from jax.experimental.pallas import tpu as pltpu
from jax.sharding import PartitionSpec as P

HD = 64
GRID = 16
F32, BF16 = jnp.float32, jnp.bfloat16
ANY = pl.BlockSpec(memory_space=pl.ANY)
VMEM = pl.BlockSpec(memory_space=pltpu.VMEM)
SMEM = pl.BlockSpec(memory_space=pltpu.SMEM)


def gelu(x):
    return jax.nn.gelu(x, approximate=True)


def params(mib):
    return pltpu.CompilerParams(vmem_limit_bytes=mib << 20)


def cost(flops, size, transcendentals=0):
    return pl.CostEstimate(
        flops=int(flops), bytes_accessed=int(size), transcendentals=int(transcendentals)
    )


def ring_of(chips):
    return list(range(0, chips, 2)) + list(range(1, chips, 2))[::-1]


def ring_positions(chips):
    steps = [0]
    for step in range(1, chips // 2 + 1):
        steps.append(-step)
        if step <= (chips - 1) // 2:
            steps.append(step)
    return steps


def gather_pieces(unit, flip):
    n = lax.axis_size("row")
    chips = n // 2
    ring = ring_of(chips)
    forward = [
        (2 * ring[i] + core, 2 * ring[(i + 1) % chips] + core)
        for i in range(chips)
        for core in (0, 1)
    ]
    backward = [(b, a) for a, b in forward]
    across = [(i, i ^ 1) for i in range(lax.axis_size("parts"))]
    turned = jnp.where(flip, unit[::-1], unit)
    own, rest = turned[:2], turned[2]
    pieces, up, down = [own], own, own
    for step in range(1, chips // 2 + 1):
        up = lax.ppermute(up, "row", forward)
        pieces.append(up)
        if step <= (chips - 1) // 2:
            down = lax.ppermute(down, "row", backward)
            pieces.append(down)
    others = pieces[1:]
    half = (len(others) + 1) // 2
    batches = [
        lax.ppermute(jnp.stack([piece[0] for piece in batch]), "parts", across)
        for batch in (others[:half], others[half:])
    ]
    return pieces + [rest] + batches


def start_copies(where, refs, target, sems):
    count = (len(refs) - 3) if len(refs) > 3 else 1
    pieces, rest, batches = refs[:count], refs[count], refs[count + 1 :]
    first = where[0]
    share = pieces[0].shape[2]
    jobs = []
    for index, piece in enumerate(pieces):
        rows = pl.ds(pl.multiple_of(where[1 + index] * share, share), share)
        jobs.append((piece.at[0], target.at[first, :, rows, :]))
        jobs.append((piece.at[1], target.at[1, :, rows, :]))
        if index == 0:
            jobs.append((rest, target.at[2 - first, :, rows, :]))
        else:
            place = index - 1
            batch = batches[0]
            if place >= batch.shape[0]:
                place -= batch.shape[0]
                batch = batches[1]
            jobs.append((batch.at[place], target.at[2 - first, :, rows, :]))
    copies = [
        pltpu.make_async_copy(source, dest, sems.at[i]) for i, (source, dest) in enumerate(jobs)
    ]
    for copy in copies:
        copy.start()
    return copies


def assemble_kernel(where, *refs):
    target, sems = refs[-2:]
    for copy in start_copies(where, refs[:-2], target, sems):
        copy.wait()


def assemble(where, pieces, chips):
    share, outs = pieces[0].shape[2:]
    shape = (3, 3, share * chips, outs)
    return pl.pallas_call(
        assemble_kernel,
        out_shape=jax.ShapeDtypeStruct(shape, BF16),
        in_specs=[SMEM] + [ANY] * len(pieces),
        out_specs=ANY,
        scratch_shapes=[pltpu.SemaphoreType.DMA((3 * chips,))],
        cost_estimate=cost(0, 4 * 9 * share * chips * outs),
        name="assemble",
    )(where, *pieces)


def conv_rows(lefts, weights, depths, row, rows, cols):
    total = []
    for b in range(3):
        part = None
        for a in range(3):
            for left, depth in zip(lefts, depths):
                block = left(row + a, rows).reshape(rows * cols, -1)
                term = jnp.dot(block, weights[a, b, depth, :], preferred_element_type=F32)
                part = term if part is None else part + term
        total.append(part)
    size = rows * cols
    col = lax.broadcasted_iota(jnp.int32, total[0].shape, 0) % cols
    left = jnp.where(col == 0, 0.0, pltpu.roll(total[0], 1, 0))
    right = jnp.where(col == cols - 1, 0.0, pltpu.roll(total[2], size - 1, 0))
    return left + total[1] + right


def first_conv_kernel(step, where, act, lat, *refs):
    pieces, (y_out, act_out, weights, sems) = refs[:-4], refs[-4:]
    copies = start_copies(where, pieces, weights, sems)
    core, top, bottom = where[where.shape[0] - 3], where[where.shape[0] - 2], where[where.shape[0] - 1]
    rows, cols, half = y_out.shape
    lanes = pl.ds(pl.multiple_of(core * half, half), half)
    for copy in copies:
        copy.wait()

    def body(i, carry):
        row = i * step
        mixed = conv_rows(
            [lambda r, k: act[pl.ds(r, k)]], weights, [slice(None)], row, step, cols
        ).reshape(step, cols, half)
        y = (lat[pl.ds(row + 1, step), :, lanes].astype(F32) + mixed).astype(BF16)
        y_out[pl.ds(row, step)] = y
        active = gelu(y.astype(F32))
        place = row + lax.broadcasted_iota(jnp.int32, active.shape, 0)
        active = jnp.where((place >= top) & (place < bottom), active, 0.0)
        act_out[pl.ds(row, step)] = active.astype(BF16)
        return carry

    lax.fori_loop(0, rows // step, body, 0)


def first_conv(where, act, lat, pieces, step):
    total_rows, cols, channels = act.shape
    rows, half, chips = total_rows - 2, channels // 2, channels // pieces[0].shape[2]
    out = jax.ShapeDtypeStruct((rows, cols, half), BF16)
    return pl.pallas_call(
        functools.partial(first_conv_kernel, step),
        out_shape=(out, out),
        in_specs=[SMEM, VMEM, VMEM] + [ANY] * len(pieces),
        out_specs=(VMEM, VMEM),
        scratch_shapes=[
            pltpu.VMEM((3, 3, channels, half), BF16),
            pltpu.SemaphoreType.DMA((3 * chips,)),
        ],
        compiler_params=params(40),
        cost_estimate=cost(
            18 * rows * cols * channels * half, 18 * channels * half, rows * cols * half
        ),
        name="first_conv",
    )(where, act, lat, *pieces)


def second_conv_kernel(step, where, y1, mine, theirs, *refs):
    pieces, (send, weights, sems, spread) = refs[:-4], refs[-4:]
    copies = start_copies(where, pieces, weights, sems)
    core = where[where.shape[0] - 3]
    groups, rows, _, half = send.shape
    cols = mine.shape[1]
    own = pl.ds(pl.multiple_of(core * half, half), half)
    other = pl.ds(pl.multiple_of((1 - core) * half, half), half)
    for copy in copies:
        copy.wait()
    lefts = [lambda r, k: mine[pl.ds(r, k)], lambda r, k: theirs[pl.ds(r, k)]]
    for row in range(0, rows, step):
        mixed = conv_rows(lefts, weights, [own, other], row, step, cols)
        before = y1[pl.ds(row + 1, step)].reshape(step * cols, half).astype(F32)
        rounded = (before + mixed).astype(BF16).astype(F32)
        for lane in range(0, half, 128):
            spread[...] = rounded[:, lane : lane + 128]
            for r in range(step):
                for c in range(groups):
                    send[c, row + r, :, lane : lane + 128] = spread[
                        pl.ds(r * cols + c, cols // groups, stride=groups), :
                    ].astype(BF16)


def second_conv(where, y1, mine, theirs, pieces, step):
    padded_rows, cols, half = y1.shape
    rows, channels = padded_rows - 2, 2 * half
    groups, chips = cols // GRID, channels // pieces[0].shape[2]
    return pl.pallas_call(
        functools.partial(second_conv_kernel, step),
        out_shape=jax.ShapeDtypeStruct((groups, rows, GRID, half), BF16),
        in_specs=[SMEM, VMEM, VMEM, VMEM] + [ANY] * len(pieces),
        out_specs=VMEM,
        scratch_shapes=[
            pltpu.VMEM((3, 3, channels, half), BF16),
            pltpu.SemaphoreType.DMA((3 * chips,)),
            pltpu.VMEM((step * cols, 128), F32),
        ],
        compiler_params=params(40),
        cost_estimate=cost(18 * rows * cols * channels * half, 18 * channels * half),
        name="second_conv",
    )(where, y1, mine, theirs, *pieces)


def rms_round(values):
    meansq = jnp.mean(values * values, axis=-1, keepdims=True)
    return (values * lax.rsqrt(meansq + 1e-06)).astype(BF16)


def window_kernel(picks, y2, w_query, w_key, w_value, w_out, w_in, w_down, out, edge, att, wide, thin):
    grid, per, _, channels = y2.shape
    cells = grid * GRID
    current = jnp.concatenate([y2[:, r].reshape(cells, channels) for r in range(per)], axis=0)
    current = current.astype(F32)
    normed = rms_round(current)
    dot = functools.partial(jnp.dot, preferred_element_type=F32)
    queries = (dot(normed, w_query[...]).astype(BF16) * BF16(HD**-0.5)).astype(BF16)
    keys = dot(normed, w_key[...]).astype(BF16)
    values = dot(normed, w_value[...]).astype(BF16)
    pair = 2 * HD
    low = lax.broadcasted_iota(jnp.int32, (cells, pair), 1) < HD
    zero = jnp.zeros((cells, pair), BF16)
    for r in range(per):
        for lane in range(0, channels, pair):
            spot = (slice(r * cells, (r + 1) * cells), slice(lane, lane + pair))
            query, key, value = queries[spot], keys[spot], values[spot]
            halves = []
            for keep in (jnp.where(low, query, zero), jnp.where(low, zero, query)):
                scores = lax.dot_general(
                    keep, key, (((1,), (1,)), ((), ())), preferred_element_type=F32
                )
                lifted = jnp.exp(scores - jnp.max(scores, axis=-1, keepdims=True))
                probs = lifted * (1.0 / jnp.sum(lifted, axis=-1, keepdims=True))
                halves.append(dot(probs.astype(BF16), value))
            att[spot] = jnp.where(low, halves[0], halves[1]).astype(BF16)
    current = (current + dot(att[...], w_out[...])).astype(BF16).astype(F32)
    normed = rms_round(current)
    units = w_in.shape[1]
    lowered = None
    for start in range(0, units, channels):
        span = slice(start, start + channels)
        hidden = gelu(dot(normed, w_in[:, span])).astype(BF16)
        term = dot(hidden, w_down[span, :])
        lowered = term if lowered is None else lowered + term
    latent = (current + lowered).astype(BF16)
    wide_values = latent.astype(F32)
    for r in range(per):
        out[:, r] = latent[r * cells : (r + 1) * cells].reshape(grid, GRID, channels)
    kept = grid // 2
    for lane in range(0, channels, 128):
        wide[...] = wide_values[:, lane : lane + 128]
        for d in range(edge.shape[0]):
            for r in range(per):
                first = r * cells + (grid // 4) * GRID + picks[d]
                thin[pl.ds(d * kept * per + r, kept, stride=per), :] = wide[
                    pl.ds(first, kept, stride=GRID), :
                ]
        edge[:, :, lane : lane + 128] = thin[...].astype(BF16).reshape(
            edge.shape[0], kept * per, 128
        )


def windows(picks, y2, w_query, w_key, w_value, w_out, w_in, w_down):
    grid, per, _, channels = y2.shape
    cells, units, dests = grid * GRID, w_in.shape[1], picks.shape[0]
    total = per * cells
    kept = per * grid // 2
    flops = 2 * total * channels * (4 * channels + 2 * units + 2 * cells)
    return pl.pallas_call(
        window_kernel,
        out_shape=(
            jax.ShapeDtypeStruct(y2.shape, BF16),
            jax.ShapeDtypeStruct((dests, kept, channels), BF16),
        ),
        in_specs=[SMEM] + [VMEM] * 7,
        out_specs=(VMEM, VMEM),
        scratch_shapes=[
            pltpu.VMEM((total, channels), BF16),
            pltpu.VMEM((total, 128), F32),
            pltpu.VMEM((dests * kept, 128), F32),
        ],
        compiler_params=params(40),
        cost_estimate=cost(flops, 8 * total * channels, total * (cells * 8 + units)),
        name="windows",
    )(picks, y2, w_query, w_key, w_value, w_out, w_in, w_down)


def upsample_kernel(info, arrived, mine, theirs, out, field, weights, spread, sems):
    taps, depth, half = mine.shape[0], mine.shape[2], mine.shape[3]
    core = info[0]
    copies = []
    for index, (source, side) in enumerate(((mine, core), (theirs, 1 - core))):
        lanes = pl.ds(pl.multiple_of(side * half, half), half)
        copies.append(pltpu.make_async_copy(source, weights.at[:, :, :, lanes], sems.at[index]))
    for copy in copies:
        copy.start()
    framed, rows, channels = field.shape
    width = framed - 2
    for j in range(framed):
        column = arrived[info[3 + j]]
        if j == 0:
            column = column * info[1].astype(F32).astype(BF16)
        if j == framed - 1:
            column = column * info[2].astype(F32).astype(BF16)
        field[j] = column
    for copy in copies:
        copy.wait()
    flat = field[...].reshape(framed * rows, channels)
    size = width * rows
    place = lax.broadcasted_iota(jnp.int32, (size, 128), 0) % rows
    out_cols = 2 * width
    for start in range(0, channels, 256):
        span = slice(start, start + 256)
        columns = []
        for a in range(3):
            p0, p1, p2 = [
                jnp.dot(flat, weights[a, b, :, span], preferred_element_type=F32)
                for b in range(3)
            ]
            middle = p1[rows : rows + size]
            columns.append(
                (
                    p0[:size] + middle + p2[rows : rows + size],
                    p0[rows : rows + size] + middle + p2[2 * rows : 2 * rows + size],
                )
            )
        for lane in range(0, 256, 128):
            for dj in range(2):
                c0, c1, c2 = [columns[a][dj][:, lane : lane + 128] for a in range(3)]
                above = jnp.where(place == 0, 0.0, pltpu.roll(c0, 1, 0))
                below = jnp.where(place == rows - 1, 0.0, pltpu.roll(c2, size - 1, 0))
                for di, value in enumerate((above + c1 + c2, c0 + c1 + below)):
                    for j in range(width):
                        first = di * out_cols + 2 * j + dj
                        spread[pl.ds(first, rows, stride=2 * out_cols), :] = value[
                            j * rows : (j + 1) * rows
                        ]
            out[:, :, start + lane : start + lane + 128] = (
                spread[...].astype(BF16).reshape(2 * rows, out_cols, 128)
            )


def upsample(info, arrived, mine, theirs, width):
    _, rows, channels = arrived.shape
    framed = width + 2
    return pl.pallas_call(
        upsample_kernel,
        out_shape=jax.ShapeDtypeStruct((2 * rows, 2 * width, channels), BF16),
        in_specs=[SMEM, VMEM, ANY, ANY],
        out_specs=VMEM,
        scratch_shapes=[
            pltpu.VMEM((framed, rows, channels), BF16),
            pltpu.VMEM((3, 3, channels, channels), BF16),
            pltpu.VMEM((4 * rows * width, 128), F32),
            pltpu.SemaphoreType.DMA((2,)),
        ],
        compiler_params=params(40),
        cost_estimate=cost(18 * framed * rows * channels * channels, 18 * channels * channels),
        name="upsample",
    )(info, arrived, mine, theirs)


def on_device(
    latent, conv_first, conv_second, w_query, w_key, w_value, w_out, w_in, w_down, conv_up
):
    n = lax.axis_size("row")
    chips = n // 2
    device = lax.axis_index("row")
    core, chip = device % 2, device // 2
    per, cols, channels = latent.shape
    half = channels // 2
    flip = lax.axis_index("parts") % 2 == 1
    swap = [(i, i ^ 1) for i in range(n)]

    shares = jnp.stack([conv_first, conv_second, conv_up])
    mine = lax.dynamic_slice_in_dim(shares, core * half, half, axis=4)
    given = lax.dynamic_slice_in_dim(shares, (1 - core) * half, half, axis=4)
    got = lax.ppermute(given, "row", swap)
    units = jnp.where(
        core == 0, jnp.concatenate([mine, got], axis=3), jnp.concatenate([got, mine], axis=3)
    )
    first_pieces, second_pieces, up_pieces = [gather_pieces(units[k], flip) for k in range(3)]
    ring = jnp.array(ring_of(chips), jnp.int32)
    position = jnp.argmax(ring == chip).astype(jnp.int32)
    steps = jnp.array(ring_positions(chips), jnp.int32)
    owners = ring[(position + steps) % chips]
    top = jnp.where(chip == 0, 1, 0)
    bottom = 2 * per + 2 - jnp.where(chip == chips - 1, 1, 0)
    where = jnp.concatenate(
        [jnp.where(flip, 2, 0)[None], owners, jnp.stack([core, top, bottom])]
    ).astype(jnp.int32)

    up = lax.ppermute(latent, "row", [(i, i + 1) for i in range(n - 1)])
    down = lax.ppermute(latent, "row", [(i + 1, i) for i in range(n - 1)])
    far = lax.ppermute(jnp.where(core == 0, up[-2:], down[:2]), "row", swap)
    field = jnp.where(
        core == 0,
        jnp.concatenate([up[-2:], latent, down, far], axis=0),
        jnp.concatenate([far, up, latent, down[:2]], axis=0),
    )
    active = gelu(field.astype(F32)).astype(BF16)

    y1, active2 = first_conv(where, active, field, first_pieces, 2)
    theirs = lax.ppermute(active2, "row", swap)
    y2 = second_conv(where, y1, active2, theirs, second_pieces, 2)

    groups = cols // GRID
    subs = n // groups
    index_groups = None
    if subs > 1:
        index_groups = [[k * subs + s for k in range(groups)] for s in range(subs)]
    kept = lax.dynamic_slice_in_dim(y2, core * per, per, axis=1)
    passed = lax.dynamic_slice_in_dim(y2, (1 - core) * per, per, axis=1)
    partner = lax.ppermute(passed, "row", swap)
    y2 = jnp.where(
        core == 0,
        jnp.concatenate([kept, partner], axis=3),
        jnp.concatenate([partner, kept], axis=3),
    )
    owned = lax.all_to_all(
        y2, "row", split_axis=0, concat_axis=0, axis_index_groups=index_groups, tiled=True
    )
    width = cols // 2 // n
    dests = jnp.arange(n, dtype=jnp.int32)
    starts = cols // 4 + width * dests - 1
    column = device // subs
    picks = jnp.clip((starts - column + groups - 1) // groups, 0, GRID - 1).astype(jnp.int32)
    latent_window, edge = windows(
        picks, owned, w_query, w_key, w_value, w_out, w_in, w_down
    )

    arrived = lax.all_to_all(edge, "row", split_axis=0, concat_axis=0, tiled=True)
    if subs > 1:
        arrived = arrived.reshape(groups, subs, GRID // 2, per, channels)
        arrived = arrived.transpose(0, 2, 1, 3, 4)
    arrived = arrived.reshape(groups, subs * per * GRID // 2, channels)
    returned = lax.all_to_all(
        latent_window,
        "row",
        split_axis=0,
        concat_axis=0,
        axis_index_groups=index_groups,
        tiled=True,
    )
    latent_out = returned.transpose(1, 2, 0, 3).reshape(per, cols, channels)

    up_mine = assemble(where, up_pieces, chips)
    up_theirs = lax.ppermute(up_mine, "row", swap)
    sources = (cols // 4 + width * device - 1 + jnp.arange(width + 2, dtype=jnp.int32)) % groups
    info = jnp.concatenate(
        [jnp.stack([core, (device > 0).astype(jnp.int32), (device < n - 1).astype(jnp.int32)]), sources]
    ).astype(jnp.int32)
    upsampled = upsample(info, arrived, up_mine, up_theirs, width)
    return (latent_out, upsampled)


def solution(mesh):
    placed = (
        P(("parts", "row"), None, None),
        P(None, None, "row", None),
        P(None, None, "row", None),
        P(),
        P(),
        P(),
        P(),
        P(),
        P(),
        P(None, None, "row", None),
    )
    return jax.shard_map(
        on_device,
        mesh=mesh,
        in_specs=placed,
        out_specs=(P(("parts", "row"), None, None), P("parts", "row", None)),
        check_vma=False,
    )
```

```python
import functools

import jax
import jax.numpy as jnp
from jax import lax
from jax.experimental import pallas as pl
from jax.experimental.pallas import tpu as pltpu
from jax.sharding import PartitionSpec as P

HD = 64
GRID = 16
F32, BF16 = jnp.float32, jnp.bfloat16
ANY = pl.BlockSpec(memory_space=pl.ANY)
VMEM = pl.BlockSpec(memory_space=pltpu.VMEM)
SMEM = pl.BlockSpec(memory_space=pltpu.SMEM)


def gelu(x):
    return jax.nn.gelu(x, approximate=True)


def params(mib):
    return pltpu.CompilerParams(vmem_limit_bytes=mib << 20)


def cost(flops, size, transcendentals=0):
    return pl.CostEstimate(
        flops=int(flops), bytes_accessed=int(size), transcendentals=int(transcendentals)
    )


def chip_at(position, chips):
    return jnp.where(position < chips // 2, 2 * position, 2 * (chips - 1 - position) + 1)


def ring_of(chips):
    return list(range(0, chips, 2)) + list(range(1, chips, 2))[::-1]


def ring_positions(chips):
    steps = [0]
    for step in range(1, chips // 2 + 1):
        steps.append(-step)
        if step <= (chips - 1) // 2:
            steps.append(step)
    return steps


class Gather:
    def __init__(self, unit, flip):
        turned = jnp.where(flip, unit[::-1], unit)
        self.chips = lax.axis_size("row") // 2
        self.up = self.down = turned[:2]
        self.rest = turned[2]
        self.pieces, self.finals, self.batches, self.sent = [self.up], [], [], 1

    def after(self, value):
        self.up, self.down, _ = lax.optimization_barrier((self.up, self.down, value))

    def before(self, value):
        held = (value, self.up, self.down, self.finals, self.batches[:-1])
        return lax.optimization_barrier(held)[0]

    def step(self, index):
        ring = ring_of(self.chips)
        forward = [
            (2 * ring[i] + core, 2 * ring[(i + 1) % self.chips] + core)
            for i in range(self.chips)
            for core in (0, 1)
        ]
        backward = [(b, a) for a, b in forward]
        across = [(i, i ^ 1) for i in range(lax.axis_size("parts"))]
        if index == self.chips // 2:
            ways = ((self.up, forward), (self.down, backward))
            for kernel in range(self.up.shape[1]):
                value, pairs = ways[kernel % 2]
                self.finals.append(lax.ppermute(value[:, kernel : kernel + 1], "row", pairs))
            batch = jnp.concatenate([piece[0] for piece in self.finals], axis=0)[None]
            self.batches.append(lax.ppermute(batch, "parts", across))
            return
        self.up = lax.ppermute(self.up, "row", forward)
        self.down = lax.ppermute(self.down, "row", backward)
        self.pieces += [self.up, self.down]
        count = len(self.pieces)
        if count == self.chips - 1 or count - self.sent >= self.chips // 4:
            batch = jnp.stack([piece[0] for piece in self.pieces[self.sent :]])
            self.batches.append(lax.ppermute(batch, "parts", across))
            self.sent = count

    def result(self):
        return self.pieces + self.finals + [self.rest] + self.batches


def start_copies(where, refs, index, target, sems):
    chips = target.shape[2] // refs[0].shape[3]
    near, kernels = chips - 1, refs[0].shape[1]
    finals, rest = refs[near : near + kernels], refs[near + kernels]
    batches = refs[near + kernels + 1 :]
    pieces = [piece.at[:, index] for piece in refs[:near]] + [finals[index].at[:, 0]]
    thirds = [rest.at[index]]
    for batch in batches:
        thirds += [batch.at[i, index] for i in range(batch.shape[0])]
    first = where[0]
    share = refs[0].shape[3]
    jobs = []
    for i, piece in enumerate(pieces):
        rows = pl.ds(pl.multiple_of(where[1 + i] * share, share), share)
        jobs.append((piece.at[0], target.at[first, :, rows, :]))
        jobs.append((piece.at[1], target.at[1, :, rows, :]))
        jobs.append((thirds[i], target.at[2 - first, :, rows, :]))
    copies = [
        pltpu.make_async_copy(source, dest, sems.at[i]) for i, (source, dest) in enumerate(jobs)
    ]
    for copy in copies:
        copy.start()
    return copies


def assemble_kernel(where, *refs):
    target, sems = refs[-2:]
    for copy in start_copies(where, refs[:-2], 0, target, sems):
        copy.wait()


def assemble(where, pieces, chips):
    share, outs = pieces[0].shape[3:]
    shape = (3, 3, share * chips, outs)
    return pl.pallas_call(
        assemble_kernel,
        out_shape=jax.ShapeDtypeStruct(shape, BF16),
        in_specs=[SMEM] + [ANY] * len(pieces),
        out_specs=VMEM,
        scratch_shapes=[pltpu.SemaphoreType.DMA((3 * chips,))],
        compiler_params=params(12),
        cost_estimate=cost(0, 4 * 9 * share * chips * outs),
        name="assemble",
    )(where, *pieces)


def conv_rows(lefts, weights, depths, row, rows, cols):
    total = []
    for b in range(3):
        part = None
        for a in range(3):
            for left, depth in zip(lefts, depths):
                block = left(row + a, rows).reshape(rows * cols, -1)
                term = jnp.dot(block, weights[a, b, depth, :], preferred_element_type=F32)
                part = term if part is None else part + term
        total.append(part)
    size = rows * cols
    col = lax.broadcasted_iota(jnp.int32, total[0].shape, 0) % cols
    left = jnp.where(col == 0, 0.0, pltpu.roll(total[0], 1, 0))
    right = jnp.where(col == cols - 1, 0.0, pltpu.roll(total[2], size - 1, 0))
    return left + total[1] + right


def first_conv_kernel(step, where, act, lat, *refs):
    pieces, (y_out, act_out, weights, sems) = refs[:-4], refs[-4:]
    copies = start_copies(where, pieces, 0, weights, sems)
    core, top, bottom = where[where.shape[0] - 3], where[where.shape[0] - 2], where[where.shape[0] - 1]
    rows, cols, half = y_out.shape
    lanes = pl.ds(pl.multiple_of(core * half, half), half)
    for copy in copies:
        copy.wait()

    def body(i, carry):
        row = i * step
        mixed = conv_rows(
            [lambda r, k: act[pl.ds(r, k)]], weights, [slice(None)], row, step, cols
        ).reshape(step, cols, half)
        y = (lat[pl.ds(row + 1, step), :, lanes].astype(F32) + mixed).astype(BF16)
        y_out[pl.ds(row, step)] = y
        active = gelu(y.astype(F32))
        place = row + lax.broadcasted_iota(jnp.int32, active.shape, 0)
        active = jnp.where((place >= top) & (place < bottom), active, 0.0)
        act_out[pl.ds(row, step)] = active.astype(BF16)
        return carry

    lax.fori_loop(0, rows // step, body, 0)


def first_conv(where, act, lat, pieces, step):
    total_rows, cols, channels = act.shape
    rows, half, chips = total_rows - 2, channels // 2, channels // pieces[0].shape[3]
    out = jax.ShapeDtypeStruct((rows, cols, half), BF16)
    return pl.pallas_call(
        functools.partial(first_conv_kernel, step),
        out_shape=(out, out),
        in_specs=[SMEM, VMEM, VMEM] + [ANY] * len(pieces),
        out_specs=(VMEM, VMEM),
        scratch_shapes=[
            pltpu.VMEM((3, 3, channels, half), BF16),
            pltpu.SemaphoreType.DMA((3 * chips,)),
        ],
        compiler_params=params(40),
        cost_estimate=cost(
            18 * rows * cols * channels * half, 18 * channels * half, rows * cols * half
        ),
        name="first_conv",
    )(where, act, lat, *pieces)


def second_conv_kernel(step, where, y1, mine, theirs, *refs):
    pieces, (send, weights, sems, spread) = refs[:-4], refs[-4:]
    copies = start_copies(where, pieces, 1, weights, sems)
    core = where[where.shape[0] - 3]
    groups, rows, _, half = send.shape
    cols = mine.shape[1]
    own = pl.ds(pl.multiple_of(core * half, half), half)
    other = pl.ds(pl.multiple_of((1 - core) * half, half), half)
    for copy in copies:
        copy.wait()
    lefts = [lambda r, k: mine[pl.ds(r, k)], lambda r, k: theirs[pl.ds(r, k)]]
    for row in range(0, rows, step):
        mixed = conv_rows(lefts, weights, [own, other], row, step, cols)
        before = y1[pl.ds(row + 1, step)].reshape(step * cols, half).astype(F32)
        rounded = (before + mixed).astype(BF16).astype(F32)
        for lane in range(0, half, 128):
            spread[...] = rounded[:, lane : lane + 128]
            for r in range(step):
                for c in range(groups):
                    send[c, row + r, :, lane : lane + 128] = spread[
                        pl.ds(r * cols + c, cols // groups, stride=groups), :
                    ].astype(BF16)


def second_conv(where, y1, mine, theirs, pieces, step):
    padded_rows, cols, half = y1.shape
    rows, channels = padded_rows - 2, 2 * half
    groups, chips = cols // GRID, channels // pieces[0].shape[3]
    return pl.pallas_call(
        functools.partial(second_conv_kernel, step),
        out_shape=jax.ShapeDtypeStruct((groups, rows, GRID, half), BF16),
        in_specs=[SMEM, VMEM, VMEM, VMEM] + [ANY] * len(pieces),
        out_specs=VMEM,
        scratch_shapes=[
            pltpu.VMEM((3, 3, channels, half), BF16),
            pltpu.SemaphoreType.DMA((3 * chips,)),
            pltpu.VMEM((step * cols, 128), F32),
        ],
        compiler_params=params(40),
        cost_estimate=cost(18 * rows * cols * channels * half, 18 * channels * half),
        name="second_conv",
    )(where, y1, mine, theirs, *pieces)


def rms_round(values):
    meansq = jnp.mean(values * values, axis=-1, keepdims=True)
    return (values * lax.rsqrt(meansq + 1e-06)).astype(BF16)


def window_kernel(picks, y2, *refs):
    sources, (out, edge), (att, wide, thin) = refs[:6], refs[6:8], refs[8:11]
    weights, sems = refs[11:17], refs[17]
    copies = [
        pltpu.make_async_copy(source, dest, sems.at[i])
        for i, (source, dest) in enumerate(zip(sources, weights))
    ]
    for copy in copies:
        copy.start()
    w_query, w_key, w_value, w_out, w_in, w_down = weights
    grid, per, _, channels = out.shape
    cells = grid * GRID
    current = jnp.concatenate(
        [
            jnp.concatenate(
                [y2[:, side, :, r].reshape(cells, -1) for side in range(y2.shape[1])], axis=1
            )
            for r in range(per)
        ],
        axis=0,
    ).astype(F32)
    normed = rms_round(current)
    dot = functools.partial(jnp.dot, preferred_element_type=F32)
    for copy in copies[:3]:
        copy.wait()
    queries = (dot(normed, w_query[...]).astype(BF16) * BF16(HD**-0.5)).astype(BF16)
    keys = dot(normed, w_key[...]).astype(BF16)
    values = dot(normed, w_value[...]).astype(BF16)
    pair = 2 * HD
    low = lax.broadcasted_iota(jnp.int32, (cells, pair), 1) < HD
    zero = jnp.zeros((cells, pair), BF16)
    for r in range(per):
        for lane in range(0, channels, pair):
            spot = (slice(r * cells, (r + 1) * cells), slice(lane, lane + pair))
            query, key, value = queries[spot], keys[spot], values[spot]
            halves = []
            for keep in (jnp.where(low, query, zero), jnp.where(low, zero, query)):
                scores = lax.dot_general(
                    keep, key, (((1,), (1,)), ((), ())), preferred_element_type=F32
                )
                lifted = jnp.exp(scores - jnp.max(scores, axis=-1, keepdims=True))
                probs = lifted * (1.0 / jnp.sum(lifted, axis=-1, keepdims=True))
                halves.append(dot(probs.astype(BF16), value))
            att[spot] = jnp.where(low, halves[0], halves[1]).astype(BF16)
    for copy in copies[3:]:
        copy.wait()
    current = (current + dot(att[...], w_out[...])).astype(BF16).astype(F32)
    normed = rms_round(current)
    units = w_in.shape[1]
    lowered = None
    for start in range(0, units, channels):
        span = slice(start, start + channels)
        hidden = gelu(dot(normed, w_in[:, span])).astype(BF16)
        term = dot(hidden, w_down[span, :])
        lowered = term if lowered is None else lowered + term
    latent = (current + lowered).astype(BF16)
    wide_values = latent.astype(F32)
    for r in range(per):
        out[:, r] = latent[r * cells : (r + 1) * cells].reshape(grid, GRID, channels)
    kept = grid // 2
    for lane in range(0, channels, 128):
        wide[...] = wide_values[:, lane : lane + 128]
        for d in range(edge.shape[0]):
            for r in range(per):
                first = r * cells + (grid // 4) * GRID + picks[d]
                thin[pl.ds(d * kept * per + r, kept, stride=per), :] = wide[
                    pl.ds(first, kept, stride=GRID), :
                ]
        edge[:, :, lane : lane + 128] = thin[...].astype(BF16).reshape(
            edge.shape[0], kept * per, 128
        )


def windows(picks, y2, w_query, w_key, w_value, w_out, w_in, w_down):
    grid, per, channels = y2.shape[0] * y2.shape[2], y2.shape[3], w_query.shape[0]
    cells, units, dests = grid * GRID, w_in.shape[1], picks.shape[0]
    total = per * cells
    kept = per * grid // 2
    flops = 2 * total * channels * (4 * channels + 2 * units + 2 * cells)
    return pl.pallas_call(
        window_kernel,
        out_shape=(
            jax.ShapeDtypeStruct((grid, per, GRID, channels), BF16),
            jax.ShapeDtypeStruct((dests, kept, channels), BF16),
        ),
        in_specs=[SMEM, VMEM] + [ANY] * 6,
        out_specs=(VMEM, VMEM),
        scratch_shapes=[
            pltpu.VMEM((total, channels), BF16),
            pltpu.VMEM((total, 128), F32),
            pltpu.VMEM((dests * kept, 128), F32),
        ]
        + [
            pltpu.VMEM(weight.shape, BF16)
            for weight in (w_query, w_key, w_value, w_out, w_in, w_down)
        ]
        + [pltpu.SemaphoreType.DMA((6,))],
        compiler_params=params(56),
        cost_estimate=cost(flops, 8 * total * channels, total * (cells * 8 + units)),
        name="windows",
    )(picks, y2, w_query, w_key, w_value, w_out, w_in, w_down)


def upsample_kernel(info, arrived, mine, theirs, out, field, weights, spread, sems):
    taps, depth, half = mine.shape[0], mine.shape[2], mine.shape[3]
    core = info[0]
    copies = []
    for index, (source, side) in enumerate(((mine, core), (theirs, 1 - core))):
        lanes = pl.ds(pl.multiple_of(side * half, half), half)
        copies.append(pltpu.make_async_copy(source, weights.at[:, :, :, lanes], sems.at[index]))
    for copy in copies:
        copy.start()
    framed, rows, channels = field.shape
    width = framed - 2
    for j in range(framed):
        column = arrived[info[3 + j]]
        if j == 0:
            column = column * info[1].astype(F32).astype(BF16)
        if j == framed - 1:
            column = column * info[2].astype(F32).astype(BF16)
        field[j] = column
    for copy in copies:
        copy.wait()
    flat = field[...].reshape(framed * rows, channels)
    size = width * rows
    place = lax.broadcasted_iota(jnp.int32, (size, 128), 0) % rows
    out_cols = 2 * width
    for start in range(0, channels, 256):
        span = slice(start, start + 256)
        columns = []
        for a in range(3):
            p0, p1, p2 = [
                jnp.dot(flat, weights[a, b, :, span], preferred_element_type=F32)
                for b in range(3)
            ]
            middle = p1[rows : rows + size]
            columns.append(
                (
                    p0[:size] + middle + p2[rows : rows + size],
                    p0[rows : rows + size] + middle + p2[2 * rows : 2 * rows + size],
                )
            )
        for lane in range(0, 256, 128):
            for dj in range(2):
                c0, c1, c2 = [columns[a][dj][:, lane : lane + 128] for a in range(3)]
                above = jnp.where(place == 0, 0.0, pltpu.roll(c0, 1, 0))
                below = jnp.where(place == rows - 1, 0.0, pltpu.roll(c2, size - 1, 0))
                for di, value in enumerate((above + c1 + c2, c0 + c1 + below)):
                    for j in range(width):
                        first = di * out_cols + 2 * j + dj
                        spread[pl.ds(first, rows, stride=2 * out_cols), :] = value[
                            j * rows : (j + 1) * rows
                        ]
            out[:, :, start + lane : start + lane + 128] = (
                spread[...].astype(BF16).reshape(2 * rows, out_cols, 128)
            )


def upsample(info, arrived, mine, theirs, width):
    _, rows, channels = arrived.shape
    framed = width + 2
    return pl.pallas_call(
        upsample_kernel,
        out_shape=jax.ShapeDtypeStruct((2 * rows, 2 * width, channels), BF16),
        in_specs=[SMEM, VMEM, ANY, ANY],
        out_specs=VMEM,
        scratch_shapes=[
            pltpu.VMEM((framed, rows, channels), BF16),
            pltpu.VMEM((3, 3, channels, channels), BF16),
            pltpu.VMEM((4 * rows * width, 128), F32),
            pltpu.SemaphoreType.DMA((2,)),
        ],
        compiler_params=params(40),
        cost_estimate=cost(18 * framed * rows * channels * channels, 18 * channels * channels),
        name="upsample",
    )(info, arrived, mine, theirs)


def settle_kernel(arrived, earlier, out, spread):
    groups, per, cells, channels = arrived.shape
    for r in range(per):
        for lane in range(0, channels, 128):
            for c in range(groups):
                spread[pl.ds(c, cells, stride=groups), :] = arrived[
                    c, r, :, lane : lane + 128
                ].astype(F32)
            out[r, :, lane : lane + 128] = spread[...].astype(BF16)


def settle(arrived, earlier):
    groups, per, cells, channels = arrived.shape
    return pl.pallas_call(
        settle_kernel,
        out_shape=jax.ShapeDtypeStruct((per, groups * cells, channels), BF16),
        in_specs=[VMEM, ANY],
        out_specs=VMEM,
        scratch_shapes=[pltpu.VMEM((groups * cells, 128), F32)],
        compiler_params=params(8),
        name="settle",
    )(arrived, earlier)


def on_device(
    latent, conv_first, conv_second, w_query, w_key, w_value, w_out, w_in, w_down, conv_up
):
    n = lax.axis_size("row")
    chips = n // 2
    device = lax.axis_index("row")
    core, chip = device % 2, device // 2
    per, cols, channels = latent.shape
    half = channels // 2
    flip = lax.axis_index("parts") % 2 == 1
    swap = [(i, i ^ 1) for i in range(n)]

    def unit_of(share):
        mine = lax.dynamic_slice_in_dim(share, core * half, half, axis=share.ndim - 1)
        given = lax.dynamic_slice_in_dim(share, (1 - core) * half, half, axis=share.ndim - 1)
        got = lax.ppermute(given, "row", swap)
        depth = share.ndim - 2
        return jnp.where(
            core == 0,
            jnp.concatenate([mine, got], axis=depth),
            jnp.concatenate([got, mine], axis=depth),
        )

    pair = Gather(unit_of(jnp.stack([conv_first, conv_second], axis=1)), flip)
    latent_later, conv_later, _ = lax.optimization_barrier((latent, conv_up, pair.up))
    last = Gather(unit_of(conv_later[:, None]), flip)

    edges = []
    for i in range(chips - 1):
        edges += [(2 * i + 1, 2 * i + 2), (2 * i + 2, 2 * i + 1)]
    beside = jnp.where(core == 0, latent_later[:2], latent_later[-2:])
    near = lax.ppermute(beside, "row", edges)
    partner = lax.ppermute(latent_later, "row", swap)
    count = chips // 2
    for index in range(1, count):
        if len(pair.batches) > 1:
            pair.after(pair.batches[-2])
        pair.step(index)
    near_later, _ = lax.optimization_barrier((near, pair.up))
    far = lax.ppermute(near_later, "row", swap)
    pair.after(pair.batches[-2])
    pair.step(count)
    last.after(pair.finals)
    last.step(1)
    field = jnp.where(
        core == 0,
        jnp.concatenate([near, latent, partner, far], axis=0),
        jnp.concatenate([far, partner, latent, near], axis=0),
    )
    active = last.before(gelu(field.astype(F32)).astype(BF16))
    last.after(active)
    last.step(2)

    place = jnp.where(chip % 2 == 0, chip // 2, chips - 1 - chip // 2)
    owners = chip_at((place + jnp.array(ring_positions(chips), jnp.int32)) % chips, chips)
    top = jnp.where(chip == 0, 1, 0)
    bottom = 2 * per + 2 - jnp.where(chip == chips - 1, 1, 0)
    where = jnp.concatenate(
        [jnp.where(flip, 2, 0)[None], owners, jnp.stack([core, top, bottom])]
    ).astype(jnp.int32)

    y1, active2 = first_conv(where, active, field, pair.result(), 2)
    active2 = last.before(active2)
    theirs = lax.ppermute(active2, "row", swap)
    last.after(active2)
    last.step(3)
    y2 = second_conv(where, y1, active2, theirs, pair.result(), 2)

    y2 = last.before(y2)
    groups = cols // GRID
    subs = n // groups
    index_groups = None
    if subs > 1:
        index_groups = [[k * subs + s for k in range(groups)] for s in range(subs)]
    if subs > 1:
        kept = lax.dynamic_slice_in_dim(y2, core * per, per, axis=1)
        passed = lax.dynamic_slice_in_dim(y2, (1 - core) * per, per, axis=1)
        partner = lax.ppermute(passed, "row", swap)
        y2 = jnp.where(
            core == 0,
            jnp.concatenate([kept, partner], axis=3),
            jnp.concatenate([partner, kept], axis=3),
        )
    owned = lax.all_to_all(
        y2, "row", split_axis=0, concat_axis=0, axis_index_groups=index_groups, tiled=True
    )
    last.after(owned)
    for index in range(4, count + 1):
        last.step(index)
    sides = 2 if subs == 1 else 1
    owned = owned.reshape(GRID // 2, sides, 2, per, GRID, channels // sides)
    width = cols // 2 // n
    dests = jnp.arange(n, dtype=jnp.int32)
    starts = cols // 4 + width * dests - 1
    column = device // subs
    picks = jnp.clip((starts - column + groups - 1) // groups, 0, GRID - 1).astype(jnp.int32)
    latent_window, edge = windows(
        picks, owned, w_query, w_key, w_value, w_out, w_in, w_down
    )

    edge = last.before(edge)
    edge = edge.reshape(n, per, -1, channels)
    arrived = lax.all_to_all(edge, "row", split_axis=0, concat_axis=0, tiled=True)
    arrived, latent_window = lax.optimization_barrier((arrived, latent_window))
    if subs > 1:
        arrived = arrived.reshape(groups, subs, GRID // 2, per, channels)
        arrived = arrived.transpose(0, 2, 1, 3, 4)
    arrived = arrived.reshape(groups, subs * per * GRID // 2, channels)
    returned = lax.all_to_all(
        latent_window,
        "row",
        split_axis=0,
        concat_axis=0,
        axis_index_groups=index_groups,
        tiled=True,
    )
    where_later = lax.optimization_barrier((where, edge))[0]
    up_mine = assemble(where_later, last.result(), chips)
    up_theirs = lax.ppermute(up_mine, "row", swap)
    sources = (cols // 4 + width * device - 1 + jnp.arange(width + 2, dtype=jnp.int32)) % groups
    info = jnp.concatenate(
        [jnp.stack([core, (device > 0).astype(jnp.int32), (device < n - 1).astype(jnp.int32)]), sources]
    ).astype(jnp.int32)
    upsampled = upsample(info, arrived, up_mine, up_theirs, width)
    return (settle(returned, upsampled), upsampled)


def solution(mesh):
    placed = (
        P(("parts", "row"), None, None),
        P(None, None, "row", None),
        P(None, None, "row", None),
        P(),
        P(),
        P(),
        P(),
        P(),
        P(),
        P(None, None, "row", None),
    )
    return jax.shard_map(
        on_device,
        mesh=mesh,
        in_specs=placed,
        out_specs=(P(("parts", "row"), None, None), P("parts", "row", None)),
        check_vma=False,
    )
```

```python
import functools

import jax
import jax.numpy as jnp
from jax import lax
from jax.experimental import pallas as pl
from jax.experimental.pallas import tpu as pltpu
from jax.sharding import PartitionSpec as P

HD = 64
GRID = 16
F32, BF16 = jnp.float32, jnp.bfloat16
ANY = pl.BlockSpec(memory_space=pl.ANY)
VMEM = pl.BlockSpec(memory_space=pltpu.VMEM)
SMEM = pl.BlockSpec(memory_space=pltpu.SMEM)


def gelu(x):
    return jax.nn.gelu(x, approximate=True)


def params(mib):
    return pltpu.CompilerParams(vmem_limit_bytes=mib << 20)


def cost(flops, size, transcendentals=0):
    return pl.CostEstimate(
        flops=int(flops), bytes_accessed=int(size), transcendentals=int(transcendentals)
    )


def chip_at(position, chips):
    return jnp.where(position < chips // 2, 2 * position, 2 * (chips - 1 - position) + 1)


def ring_of(chips):
    return list(range(0, chips, 2)) + list(range(1, chips, 2))[::-1]


def ring_positions(chips):
    steps = [0]
    for step in range(1, chips // 2 + 1):
        steps.append(-step)
        if step <= (chips - 1) // 2:
            steps.append(step)
    return steps


class Gather:
    def __init__(self, unit, flip, whole):
        turned = jnp.where(flip, unit[::-1], unit)
        self.chips, self.whole = lax.axis_size("row") // 2, whole
        self.up = self.down = turned[:2]
        self.rest = turned[2]
        self.pieces, self.finals, self.batches, self.sent = [self.up], [], [], 1

    def after(self, value):
        self.up, self.down, _ = lax.optimization_barrier((self.up, self.down, value))

    def before(self, value):
        held = (value, self.up, self.down, self.finals, self.batches[:-1])
        return lax.optimization_barrier(held)[0]

    def step(self, index):
        ring = ring_of(self.chips)
        forward = [
            (2 * ring[i] + core, 2 * ring[(i + 1) % self.chips] + core)
            for i in range(self.chips)
            for core in (0, 1)
        ]
        backward = [(b, a) for a, b in forward]
        across = [(i, i ^ 1) for i in range(lax.axis_size("parts"))]
        if index == self.chips // 2:
            ways = ((self.up, forward), (self.down, backward))
            for kernel in range(self.up.shape[1]):
                value, pairs = ways[kernel % 2]
                self.finals.append(lax.ppermute(value[:, kernel : kernel + 1], "row", pairs))
            return
        self.up = lax.ppermute(self.up, "row", forward)
        self.down = lax.ppermute(self.down, "row", backward)
        self.pieces += [self.up, self.down]
        near = len(self.pieces) < self.chips - 1
        if (near and len(self.pieces) - self.sent >= self.chips // 4) or (not near and self.whole):
            self.cross(slice(None))

    def cross(self, kernels):
        across = [(i, i ^ 1) for i in range(lax.axis_size("parts"))]
        thirds = [piece[0, kernels] for piece in self.pieces[self.sent :]]
        self.batches.append(lax.ppermute(jnp.stack(thirds), "parts", across))
        self.sent = len(self.pieces)

    def cross_final(self, kernel):
        across = [(i, i ^ 1) for i in range(lax.axis_size("parts"))]
        self.batches.append(lax.ppermute(self.finals[kernel][:1], "parts", across))

    def cross_late(self, kernel, since):
        across = [(i, i ^ 1) for i in range(lax.axis_size("parts"))]
        late = self.pieces[since:] + self.finals[kernel : kernel + 1]
        thirds = [piece[0, -1:] for piece in late]
        return lax.ppermute(jnp.stack(thirds), "parts", across)

    def result(self):
        return self.pieces + self.finals + [self.rest] + self.batches


def start_copies(where, refs, index, target, sems):
    chips = target.shape[2] // refs[0].shape[3]
    near, kernels = chips - 1, refs[0].shape[1]
    finals, rest = refs[near : near + kernels], refs[near + kernels]
    batches = refs[near + kernels + 1 :]
    pieces = [piece.at[:, index] for piece in refs[:near]] + [finals[index].at[:, 0]]
    thirds = [rest.at[index]]
    for batch in batches:
        kernel = min(index, batch.shape[1] - 1)
        thirds += [batch.at[i, kernel] for i in range(batch.shape[0])]
    first = where[0]
    share = refs[0].shape[3]
    jobs = []
    for i, piece in enumerate(pieces):
        rows = pl.ds(pl.multiple_of(where[1 + i] * share, share), share)
        jobs.append((piece.at[0], target.at[first, :, rows, :]))
        jobs.append((piece.at[1], target.at[1, :, rows, :]))
        jobs.append((thirds[i], target.at[2 - first, :, rows, :]))
    copies = [
        pltpu.make_async_copy(source, dest, sems.at[i]) for i, (source, dest) in enumerate(jobs)
    ]
    for copy in copies:
        copy.start()
    return copies


def assemble_kernel(where, *refs):
    target, sems = refs[-2:]
    for copy in start_copies(where, refs[:-2], 0, target, sems):
        copy.wait()


def assemble(where, pieces, chips):
    share, outs = pieces[0].shape[3:]
    shape = (3, 3, share * chips, outs)
    return pl.pallas_call(
        assemble_kernel,
        out_shape=jax.ShapeDtypeStruct(shape, BF16),
        in_specs=[SMEM] + [ANY] * len(pieces),
        out_specs=VMEM,
        scratch_shapes=[pltpu.SemaphoreType.DMA((3 * chips,))],
        compiler_params=params(12),
        cost_estimate=cost(0, 4 * 9 * share * chips * outs),
        name="assemble",
    )(where, *pieces)


def conv_rows(lefts, weights, depths, row, rows, cols):
    total = []
    for b in range(3):
        part = None
        for a in range(3):
            for left, depth in zip(lefts, depths):
                block = left(row + a, rows).reshape(rows * cols, -1)
                term = jnp.dot(block, weights[a, b, depth, :], preferred_element_type=F32)
                part = term if part is None else part + term
        total.append(part)
    size = rows * cols
    col = lax.broadcasted_iota(jnp.int32, total[0].shape, 0) % cols
    left = jnp.where(col == 0, 0.0, pltpu.roll(total[0], 1, 0))
    right = jnp.where(col == cols - 1, 0.0, pltpu.roll(total[2], size - 1, 0))
    return left + total[1] + right


def first_conv_kernel(step, where, act, lat, *refs):
    pieces, (y_out, act_out, weights, sems) = refs[:-4], refs[-4:]
    copies = start_copies(where, pieces, 0, weights, sems)
    core, top, bottom = where[where.shape[0] - 3], where[where.shape[0] - 2], where[where.shape[0] - 1]
    rows, cols, half = y_out.shape
    lanes = pl.ds(pl.multiple_of(core * half, half), half)
    for copy in copies:
        copy.wait()

    def body(i, carry):
        row = i * step
        mixed = conv_rows(
            [lambda r, k: act[pl.ds(r, k)]], weights, [slice(None)], row, step, cols
        ).reshape(step, cols, half)
        y = (lat[pl.ds(row + 1, step), :, lanes].astype(F32) + mixed).astype(BF16)
        y_out[pl.ds(row, step)] = y
        active = gelu(y.astype(F32))
        place = row + lax.broadcasted_iota(jnp.int32, active.shape, 0)
        active = jnp.where((place >= top) & (place < bottom), active, 0.0)
        act_out[pl.ds(row, step)] = active.astype(BF16)
        return carry

    lax.fori_loop(0, rows // step, body, 0)


def first_conv(where, act, lat, pieces, step):
    total_rows, cols, channels = act.shape
    rows, half, chips = total_rows - 2, channels // 2, channels // pieces[0].shape[3]
    out = jax.ShapeDtypeStruct((rows, cols, half), BF16)
    return pl.pallas_call(
        functools.partial(first_conv_kernel, step),
        out_shape=(out, out),
        in_specs=[SMEM, VMEM, VMEM] + [ANY] * len(pieces),
        out_specs=(VMEM, VMEM),
        scratch_shapes=[
            pltpu.VMEM((3, 3, channels, half), BF16),
            pltpu.SemaphoreType.DMA((3 * chips,)),
        ],
        compiler_params=params(40),
        cost_estimate=cost(
            18 * rows * cols * channels * half, 18 * channels * half, rows * cols * half
        ),
        name="first_conv",
    )(where, act, lat, *pieces)


def second_conv_kernel(step, where, y1, mine, theirs, *refs):
    pieces, (send, weights, sems, spread) = refs[:-4], refs[-4:]
    copies = start_copies(where, pieces, 1, weights, sems)
    core = where[where.shape[0] - 3]
    groups, rows, _, half = send.shape
    cols = mine.shape[1]
    own = pl.ds(pl.multiple_of(core * half, half), half)
    other = pl.ds(pl.multiple_of((1 - core) * half, half), half)
    for copy in copies:
        copy.wait()
    lefts = [lambda r, k: mine[pl.ds(r, k)], lambda r, k: theirs[pl.ds(r, k)]]
    for row in range(0, rows, step):
        mixed = conv_rows(lefts, weights, [own, other], row, step, cols)
        before = y1[pl.ds(row + 1, step)].reshape(step * cols, half).astype(F32)
        rounded = (before + mixed).astype(BF16).astype(F32)
        for lane in range(0, half, 128):
            spread[...] = rounded[:, lane : lane + 128]
            for r in range(step):
                for c in range(groups):
                    send[c, row + r, :, lane : lane + 128] = spread[
                        pl.ds(r * cols + c, cols // groups, stride=groups), :
                    ].astype(BF16)


def second_conv(where, y1, mine, theirs, pieces, step):
    padded_rows, cols, half = y1.shape
    rows, channels = padded_rows - 2, 2 * half
    groups, chips = cols // GRID, channels // pieces[0].shape[3]
    return pl.pallas_call(
        functools.partial(second_conv_kernel, step),
        out_shape=jax.ShapeDtypeStruct((groups, rows, GRID, half), BF16),
        in_specs=[SMEM, VMEM, VMEM, VMEM] + [ANY] * len(pieces),
        out_specs=VMEM,
        scratch_shapes=[
            pltpu.VMEM((3, 3, channels, half), BF16),
            pltpu.SemaphoreType.DMA((3 * chips,)),
            pltpu.VMEM((step * cols, 128), F32),
        ],
        compiler_params=params(40),
        cost_estimate=cost(18 * rows * cols * channels * half, 18 * channels * half),
        name="second_conv",
    )(where, y1, mine, theirs, *pieces)


def rms_round(values):
    meansq = jnp.mean(values * values, axis=-1, keepdims=True)
    return (values * lax.rsqrt(meansq + 1e-06)).astype(BF16)


def window_kernel(per, picks, y2, *refs):
    sources, outs, sems = refs[:6], refs[6:-10], refs[-1]
    (att, wide, thin), weights = refs[-10:-7], refs[-7:-1]
    out, edge = outs[0], outs[-1]
    copies = [
        pltpu.make_async_copy(source, dest, sems.at[i])
        for i, (source, dest) in enumerate(zip(sources, weights))
    ]
    for copy in copies:
        copy.start()
    w_query, w_key, w_value, w_out, w_in, w_down = weights
    grid, channels = out.shape[0], out.shape[2]
    cells = grid * GRID
    current = jnp.concatenate(
        [
            jnp.concatenate(
                [y2[:, side, :, r].reshape(cells, -1) for side in range(y2.shape[1])], axis=1
            )
            for r in range(per)
        ],
        axis=0,
    ).astype(F32)
    normed = rms_round(current)
    dot = functools.partial(jnp.dot, preferred_element_type=F32)
    for copy in copies[:3]:
        copy.wait()
    queries = (dot(normed, w_query[...]).astype(BF16) * BF16(HD**-0.5)).astype(BF16)
    keys = dot(normed, w_key[...]).astype(BF16)
    values = dot(normed, w_value[...]).astype(BF16)
    pair = 2 * HD
    low = lax.broadcasted_iota(jnp.int32, (cells, pair), 1) < HD
    zero = jnp.zeros((cells, pair), BF16)
    for r in range(per):
        for lane in range(0, channels, pair):
            spot = (slice(r * cells, (r + 1) * cells), slice(lane, lane + pair))
            query, key, value = queries[spot], keys[spot], values[spot]
            halves = []
            for keep in (jnp.where(low, query, zero), jnp.where(low, zero, query)):
                scores = lax.dot_general(
                    keep, key, (((1,), (1,)), ((), ())), preferred_element_type=F32
                )
                lifted = jnp.exp(scores - jnp.max(scores, axis=-1, keepdims=True))
                probs = lifted * (1.0 / jnp.sum(lifted, axis=-1, keepdims=True))
                halves.append(dot(probs.astype(BF16), value))
            att[spot] = jnp.where(low, halves[0], halves[1]).astype(BF16)
    for copy in copies[3:]:
        copy.wait()
    current = (current + dot(att[...], w_out[...])).astype(BF16).astype(F32)
    normed = rms_round(current)
    units = w_in.shape[1]
    lowered = None
    for start in range(0, units, channels):
        span = slice(start, start + channels)
        hidden = gelu(dot(normed, w_in[:, span])).astype(BF16)
        term = dot(hidden, w_down[span, :])
        lowered = term if lowered is None else lowered + term
    latent = (current + lowered).astype(BF16)
    wide_values = latent.astype(F32)
    for r in range(per):
        out[:, r * GRID : (r + 1) * GRID] = latent[r * cells : (r + 1) * cells].reshape(
            grid, GRID, channels
        )
    kept = grid // 2
    for lane in range(0, channels, 128):
        wide[...] = wide_values[:, lane : lane + 128]
        for d in range(picks.shape[0]):
            for r in range(per):
                first = r * cells + (grid // 4) * GRID + picks[d]
                thin[pl.ds(d * kept * per + r, kept, stride=per), :] = wide[
                    pl.ds(first, kept, stride=GRID), :
                ]
        edge[:, edge.shape[1] - kept * per :, lane : lane + 128] = (
            thin[...].astype(BF16).reshape(picks.shape[0], kept * per, 128)
        )


def windows(joined, picks, y2, w_query, w_key, w_value, w_out, w_in, w_down):
    grid, per, channels = y2.shape[0] * y2.shape[2], y2.shape[3], w_query.shape[0]
    cells, units, dests = grid * GRID, w_in.shape[1], picks.shape[0]
    total = per * cells
    kept = per * grid // 2
    flops = 2 * total * channels * (4 * channels + 2 * units + 2 * cells)
    shapes = [(grid, per * GRID, channels), (dests, kept, channels)]
    if joined:
        shapes = [(grid, per * GRID + kept, channels)]
    return pl.pallas_call(
        functools.partial(window_kernel, per),
        out_shape=tuple(jax.ShapeDtypeStruct(shape, BF16) for shape in shapes),
        in_specs=[SMEM, VMEM] + [ANY] * 6,
        out_specs=tuple(VMEM for _ in shapes),
        scratch_shapes=[
            pltpu.VMEM((total, channels), BF16),
            pltpu.VMEM((total, 128), F32),
            pltpu.VMEM((dests * kept, 128), F32),
        ]
        + [
            pltpu.VMEM(weight.shape, BF16)
            for weight in (w_query, w_key, w_value, w_out, w_in, w_down)
        ]
        + [pltpu.SemaphoreType.DMA((6,))],
        compiler_params=params(56),
        cost_estimate=cost(flops, 8 * total * channels, total * (cells * 8 + units)),
        name="windows",
    )(picks, y2, w_query, w_key, w_value, w_out, w_in, w_down)


def upsample_kernel(info, arrived, mine, theirs, out, field, weights, spread, sems):
    taps, depth, half = mine.shape[0], mine.shape[2], mine.shape[3]
    core = info[0]
    copies = []
    for index, (source, side) in enumerate(((mine, core), (theirs, 1 - core))):
        lanes = pl.ds(pl.multiple_of(side * half, half), half)
        copies.append(pltpu.make_async_copy(source, weights.at[:, :, :, lanes], sems.at[index]))
    for copy in copies:
        copy.start()
    framed, rows, channels = field.shape
    width = framed - 2
    for j in range(framed):
        column = arrived[info[3 + j], pl.ds(arrived.shape[1] - rows, rows)]
        if j == 0:
            column = column * info[1].astype(F32).astype(BF16)
        if j == framed - 1:
            column = column * info[2].astype(F32).astype(BF16)
        field[j] = column
    for copy in copies:
        copy.wait()
    flat = field[...].reshape(framed * rows, channels)
    size = width * rows
    place = lax.broadcasted_iota(jnp.int32, (size, 128), 0) % rows
    out_cols = 2 * width
    for start in range(0, channels, 256):
        span = slice(start, start + 256)
        columns = []
        for a in range(3):
            p0, p1, p2 = [
                jnp.dot(flat, weights[a, b, :, span], preferred_element_type=F32)
                for b in range(3)
            ]
            middle = p1[rows : rows + size]
            columns.append(
                (
                    p0[:size] + middle + p2[rows : rows + size],
                    p0[rows : rows + size] + middle + p2[2 * rows : 2 * rows + size],
                )
            )
        for lane in range(0, 256, 128):
            for dj in range(2):
                c0, c1, c2 = [columns[a][dj][:, lane : lane + 128] for a in range(3)]
                above = jnp.where(place == 0, 0.0, pltpu.roll(c0, 1, 0))
                below = jnp.where(place == rows - 1, 0.0, pltpu.roll(c2, size - 1, 0))
                for di, value in enumerate((above + c1 + c2, c0 + c1 + below)):
                    for j in range(width):
                        first = di * out_cols + 2 * j + dj
                        spread[pl.ds(first, rows, stride=2 * out_cols), :] = value[
                            j * rows : (j + 1) * rows
                        ]
            out[:, :, start + lane : start + lane + 128] = (
                spread[...].astype(BF16).reshape(2 * rows, out_cols, 128)
            )


def upsample(info, arrived, mine, theirs, rows, width):
    channels = arrived.shape[2]
    framed = width + 2
    return pl.pallas_call(
        upsample_kernel,
        out_shape=jax.ShapeDtypeStruct((2 * rows, 2 * width, channels), BF16),
        in_specs=[SMEM, VMEM, ANY, ANY],
        out_specs=VMEM,
        scratch_shapes=[
            pltpu.VMEM((framed, rows, channels), BF16),
            pltpu.VMEM((3, 3, channels, channels), BF16),
            pltpu.VMEM((4 * rows * width, 128), F32),
            pltpu.SemaphoreType.DMA((2,)),
        ],
        compiler_params=params(40),
        cost_estimate=cost(18 * framed * rows * channels * channels, 18 * channels * channels),
        name="upsample",
    )(info, arrived, mine, theirs)


def settle_kernel(arrived, earlier, out, spread):
    per, _, channels = out.shape
    groups = arrived.shape[0]
    cells = out.shape[1] // groups
    for r in range(per):
        for lane in range(0, channels, 128):
            for c in range(groups):
                spread[pl.ds(c, cells, stride=groups), :] = arrived[
                    c, r * cells : (r + 1) * cells, lane : lane + 128
                ].astype(F32)
            out[r, :, lane : lane + 128] = spread[...].astype(BF16)


def settle(arrived, earlier, per):
    groups, cells, channels = arrived.shape[0], GRID, arrived.shape[2]
    return pl.pallas_call(
        settle_kernel,
        out_shape=jax.ShapeDtypeStruct((per, groups * cells, channels), BF16),
        in_specs=[VMEM, ANY],
        out_specs=VMEM,
        scratch_shapes=[pltpu.VMEM((groups * cells, 128), F32)],
        compiler_params=params(8),
        name="settle",
    )(arrived, earlier)


def on_device(
    latent, conv_first, conv_second, w_query, w_key, w_value, w_out, w_in, w_down, conv_up
):
    n = lax.axis_size("row")
    chips = n // 2
    device = lax.axis_index("row")
    core, chip = device % 2, device // 2
    per, cols, channels = latent.shape
    half = channels // 2
    flip = lax.axis_index("parts") % 2 == 1
    swap = [(i, i ^ 1) for i in range(n)]

    def unit_of(share):
        mine = lax.dynamic_slice_in_dim(share, core * half, half, axis=share.ndim - 1)
        given = lax.dynamic_slice_in_dim(share, (1 - core) * half, half, axis=share.ndim - 1)
        got = lax.ppermute(given, "row", swap)
        depth = share.ndim - 2
        return jnp.where(
            core == 0,
            jnp.concatenate([mine, got], axis=depth),
            jnp.concatenate([got, mine], axis=depth),
        )

    units = unit_of(jnp.stack([conv_first, conv_second, conv_up], axis=1))
    pair, last = Gather(units[:, :2], flip, False), Gather(units[:, 2:], flip, True)
    count = chips // 2
    pair.step(1)
    latent_later, _ = lax.optimization_barrier((latent, pair.up))

    edges = []
    for i in range(chips - 1):
        edges += [(2 * i + 1, 2 * i + 2), (2 * i + 2, 2 * i + 1)]
    beside = jnp.where(core == 0, latent_later[:2], latent_later[-2:])
    near = lax.ppermute(beside, "row", edges)
    partner = lax.ppermute(latent_later, "row", swap)
    far = lax.ppermute(near, "row", swap)
    for index in range(2, count):
        if len(pair.batches) > 1:
            pair.after(pair.batches[-2])
        pair.step(index)
    since, joint = pair.sent, list(pair.batches)
    pair.cross(slice(0, 1))
    last.after(pair.up)
    last.step(1)
    pair.after((joint[-1], near))
    pair.step(count)
    pair.finals = last.before(pair.finals)
    pair.cross_final(0)
    field = jnp.where(
        core == 0,
        jnp.concatenate([near, latent, partner, far], axis=0),
        jnp.concatenate([far, partner, latent, near], axis=0),
    )
    active = gelu(field.astype(F32)).astype(BF16)
    active, pair.finals[1] = lax.optimization_barrier((active, pair.finals[1]))
    first_pieces = pair.result()
    pair.batches = joint + [pair.cross_late(1, since)]
    last.after(active)
    last.step(2)

    place = jnp.where(chip % 2 == 0, chip // 2, chips - 1 - chip // 2)
    owners = chip_at((place + jnp.array(ring_positions(chips), jnp.int32)) % chips, chips)
    top = jnp.where(chip == 0, 1, 0)
    bottom = 2 * per + 2 - jnp.where(chip == chips - 1, 1, 0)
    where = jnp.concatenate(
        [jnp.where(flip, 2, 0)[None], owners, jnp.stack([core, top, bottom])]
    ).astype(jnp.int32)

    y1, active2 = first_conv(where, active, field, first_pieces, 3)
    active2 = last.before(active2)
    active2, pair.batches = lax.optimization_barrier((active2, pair.batches))
    second_pieces = pair.result()
    theirs = lax.ppermute(active2, "row", swap)
    last.after(active2)
    last.step(3)
    y2 = second_conv(where, y1, active2, theirs, second_pieces, 4)

    y2 = last.before(y2)
    groups = cols // GRID
    subs = n // groups
    index_groups = None
    if subs > 1:
        index_groups = [[k * subs + s for k in range(groups)] for s in range(subs)]
    if subs > 1:
        kept = lax.dynamic_slice_in_dim(y2, core * per, per, axis=1)
        passed = lax.dynamic_slice_in_dim(y2, (1 - core) * per, per, axis=1)
        partner = lax.ppermute(passed, "row", swap)
        y2 = jnp.where(
            core == 0,
            jnp.concatenate([kept, partner], axis=3),
            jnp.concatenate([partner, kept], axis=3),
        )
    owned = lax.all_to_all(
        y2, "row", split_axis=0, concat_axis=0, axis_index_groups=index_groups, tiled=True
    )
    last.after(owned)
    for index in range(4, count + 1):
        last.step(index)
    sides = 2 if subs == 1 else 1
    owned = owned.reshape(GRID // 2, sides, 2, per, GRID, channels // sides)
    width = cols // 2 // n
    dests = jnp.arange(n, dtype=jnp.int32)
    starts = cols // 4 + width * dests - 1
    column = device // subs
    picks = jnp.clip((starts - column + groups - 1) // groups, 0, GRID - 1).astype(jnp.int32)
    sent = windows(subs == 1, picks, owned, w_query, w_key, w_value, w_out, w_in, w_down)

    sent = last.before(sent)
    sent, last.finals = lax.optimization_barrier((sent, last.finals))
    last.cross_final(0)
    back = lax.all_to_all(
        sent[0],
        "row",
        split_axis=0,
        concat_axis=0,
        axis_index_groups=index_groups,
        tiled=True,
    )
    central = back
    rows = subs * per * GRID // 2
    if subs > 1:
        central = lax.all_to_all(sent[1], "row", split_axis=0, concat_axis=0, tiled=True)
        central = central.reshape(groups, subs, GRID // 2, per, channels)
        central = central.transpose(0, 2, 1, 3, 4).reshape(groups, rows, channels)
    up_mine = assemble(where, last.result(), chips)
    up_theirs = lax.ppermute(up_mine, "row", swap)
    sources = (cols // 4 + width * device - 1 + jnp.arange(width + 2, dtype=jnp.int32)) % groups
    info = jnp.concatenate(
        [jnp.stack([core, (device > 0).astype(jnp.int32), (device < n - 1).astype(jnp.int32)]), sources]
    ).astype(jnp.int32)
    upsampled = upsample(info, central, up_mine, up_theirs, rows, width)
    return (settle(back, upsampled, per), upsampled)


def solution(mesh):
    placed = (
        P(("parts", "row"), None, None),
        P(None, None, "row", None),
        P(None, None, "row", None),
        P(),
        P(),
        P(),
        P(),
        P(),
        P(),
        P(None, None, "row", None),
    )
    return jax.shard_map(
        on_device,
        mesh=mesh,
        in_specs=placed,
        out_specs=(P(("parts", "row"), None, None), P("parts", "row", None)),
        check_vma=False,
    )
```

```python
import functools

import jax
import jax.numpy as jnp
from jax import lax
from jax.experimental import pallas as pl
from jax.experimental.pallas import tpu as pltpu
from jax.sharding import PartitionSpec as P

HD = 64
GRID = 16
F32, BF16 = jnp.float32, jnp.bfloat16
ANY = pl.BlockSpec(memory_space=pl.ANY)
VMEM = pl.BlockSpec(memory_space=pltpu.VMEM)
SMEM = pl.BlockSpec(memory_space=pltpu.SMEM)


def gelu(x):
    return jax.nn.gelu(x, approximate=True)


def params(mib):
    return pltpu.CompilerParams(vmem_limit_bytes=mib << 20)


def cost(flops, size, transcendentals=0):
    return pl.CostEstimate(
        flops=int(flops), bytes_accessed=int(size), transcendentals=int(transcendentals)
    )


def chip_at(position, chips):
    return jnp.where(position < chips // 2, 2 * position, 2 * (chips - 1 - position) + 1)


def ring_of(chips):
    return list(range(0, chips, 2)) + list(range(1, chips, 2))[::-1]


def ring_positions(chips):
    steps = [0]
    for step in range(1, chips // 2 + 1):
        steps.append(-step)
        if step <= (chips - 1) // 2:
            steps.append(step)
    return steps


class Gather:
    def __init__(self, unit, flip, whole):
        turned = jnp.where(flip, unit[::-1], unit)
        self.chips, self.whole = lax.axis_size("row") // 2, whole
        self.up = self.down = turned[:2]
        self.rest = turned[2]
        self.pieces, self.finals, self.batches, self.sent = [self.up], [], [], 1

    def after(self, value):
        self.up, self.down, _ = lax.optimization_barrier((self.up, self.down, value))

    def before(self, value):
        held = (value, self.up, self.down, self.finals, self.batches[:-1])
        return lax.optimization_barrier(held)[0]

    def step(self, index):
        ring = ring_of(self.chips)
        forward = [
            (2 * ring[i] + core, 2 * ring[(i + 1) % self.chips] + core)
            for i in range(self.chips)
            for core in (0, 1)
        ]
        backward = [(b, a) for a, b in forward]
        across = [(i, i ^ 1) for i in range(lax.axis_size("parts"))]
        if index == self.chips // 2:
            ways = ((self.up, forward), (self.down, backward))
            for kernel in range(self.up.shape[1]):
                value, pairs = ways[kernel % 2]
                self.finals.append(lax.ppermute(value[:, kernel : kernel + 1], "row", pairs))
            return
        self.up = lax.ppermute(self.up, "row", forward)
        self.down = lax.ppermute(self.down, "row", backward)
        self.pieces += [self.up, self.down]
        near = len(self.pieces) < self.chips - 1
        if (near and len(self.pieces) - self.sent >= self.chips // 4) or (not near and self.whole):
            self.cross(slice(None))

    def cross(self, kernels):
        across = [(i, i ^ 1) for i in range(lax.axis_size("parts"))]
        thirds = [piece[0, kernels] for piece in self.pieces[self.sent :]]
        self.batches.append(lax.ppermute(jnp.stack(thirds), "parts", across))
        self.sent = len(self.pieces)

    def cross_final(self, kernel):
        across = [(i, i ^ 1) for i in range(lax.axis_size("parts"))]
        self.batches.append(lax.ppermute(self.finals[kernel][:1], "parts", across))

    def cross_late(self, kernel, since):
        across = [(i, i ^ 1) for i in range(lax.axis_size("parts"))]
        late = self.pieces[since:] + self.finals[kernel : kernel + 1]
        thirds = [piece[0, -1:] for piece in late]
        return lax.ppermute(jnp.stack(thirds), "parts", across)

    def result(self):
        return self.pieces + self.finals + [self.rest] + self.batches


def start_copies(where, refs, index, target, sems, final=True):
    chips = target.shape[2] // refs[0].shape[3]
    near, kernels = chips - 1, refs[0].shape[1] if final else 0
    finals, rest = refs[near : near + kernels], refs[near + kernels]
    batches = refs[near + kernels + 1 :]
    pieces = [piece.at[:, index] for piece in refs[:near]]
    pieces += [piece.at[:, 0] for piece in finals[index : index + 1]]
    thirds = [rest.at[index]]
    for batch in batches:
        kernel = min(index, batch.shape[1] - 1)
        thirds += [batch.at[i, kernel] for i in range(batch.shape[0])]
    first = where[0]
    share = refs[0].shape[3]
    jobs = []
    for i, piece in enumerate(pieces):
        rows = pl.ds(pl.multiple_of(where[1 + i] * share, share), share)
        jobs.append((piece.at[0], target.at[first, :, rows, :]))
        jobs.append((piece.at[1], target.at[1, :, rows, :]))
        jobs.append((thirds[i], target.at[2 - first, :, rows, :]))
    copies = [
        pltpu.make_async_copy(source, dest, sems.at[i]) for i, (source, dest) in enumerate(jobs)
    ]
    for copy in copies:
        copy.start()
    return copies


def assemble_kernel(where, *refs):
    target, sems = refs[-2:]
    for copy in start_copies(where, refs[:-2], 0, target, sems, False):
        copy.wait()


def assemble(where, pieces, chips):
    share, outs = pieces[0].shape[3:]
    shape = (3, 3, share * chips, outs)
    return pl.pallas_call(
        assemble_kernel,
        out_shape=jax.ShapeDtypeStruct(shape, BF16),
        in_specs=[SMEM] + [ANY] * len(pieces),
        out_specs=VMEM,
        scratch_shapes=[pltpu.SemaphoreType.DMA((3 * chips,))],
        compiler_params=params(12),
        cost_estimate=cost(0, 4 * 9 * share * chips * outs),
        name="assemble",
    )(where, *pieces)


def conv_rows(lefts, weights, depths, row, rows, cols):
    total = []
    for b in range(3):
        part = None
        for a in range(3):
            for left, depth in zip(lefts, depths):
                block = left(row + a, rows).reshape(rows * cols, -1)
                term = jnp.dot(block, weights[a, b, depth, :], preferred_element_type=F32)
                part = term if part is None else part + term
        total.append(part)
    size = rows * cols
    col = lax.broadcasted_iota(jnp.int32, total[0].shape, 0) % cols
    left = jnp.where(col == 0, 0.0, pltpu.roll(total[0], 1, 0))
    right = jnp.where(col == cols - 1, 0.0, pltpu.roll(total[2], size - 1, 0))
    return left + total[1] + right


def first_conv_kernel(step, where, act, lat, *refs):
    pieces, (y_out, act_out, weights, sems) = refs[:-4], refs[-4:]
    copies = start_copies(where, pieces, 0, weights, sems)
    core, top, bottom = where[where.shape[0] - 3], where[where.shape[0] - 2], where[where.shape[0] - 1]
    rows, cols, half = y_out.shape
    lanes = pl.ds(pl.multiple_of(core * half, half), half)
    for copy in copies:
        copy.wait()

    def body(i, carry):
        row = i * step
        mixed = conv_rows(
            [lambda r, k: act[pl.ds(r, k)]], weights, [slice(None)], row, step, cols
        ).reshape(step, cols, half)
        y = (lat[pl.ds(row + 1, step), :, lanes].astype(F32) + mixed).astype(BF16)
        y_out[pl.ds(row, step)] = y
        active = gelu(y.astype(F32))
        place = row + lax.broadcasted_iota(jnp.int32, active.shape, 0)
        active = jnp.where((place >= top) & (place < bottom), active, 0.0)
        act_out[pl.ds(row, step)] = active.astype(BF16)
        return carry

    lax.fori_loop(0, rows // step, body, 0)


def first_conv(where, act, lat, pieces, step):
    total_rows, cols, channels = act.shape
    rows, half, chips = total_rows - 2, channels // 2, channels // pieces[0].shape[3]
    out = jax.ShapeDtypeStruct((rows, cols, half), BF16)
    return pl.pallas_call(
        functools.partial(first_conv_kernel, step),
        out_shape=(out, out),
        in_specs=[SMEM, VMEM, VMEM] + [ANY] * len(pieces),
        out_specs=(VMEM, VMEM),
        scratch_shapes=[
            pltpu.VMEM((3, 3, channels, half), BF16),
            pltpu.SemaphoreType.DMA((3 * chips,)),
        ],
        compiler_params=params(40),
        cost_estimate=cost(
            18 * rows * cols * channels * half, 18 * channels * half, rows * cols * half
        ),
        name="first_conv",
    )(where, act, lat, *pieces)


def second_conv_kernel(step, where, y1, mine, theirs, *refs):
    pieces, (send, weights, sems, spread) = refs[:-4], refs[-4:]
    copies = start_copies(where, pieces, 1, weights, sems)
    core = where[where.shape[0] - 3]
    groups, rows, _, half = send.shape
    cols = mine.shape[1]
    own = pl.ds(pl.multiple_of(core * half, half), half)
    other = pl.ds(pl.multiple_of((1 - core) * half, half), half)
    for copy in copies:
        copy.wait()
    lefts = [lambda r, k: mine[pl.ds(r, k)], lambda r, k: theirs[pl.ds(r, k)]]
    for row in range(0, rows, step):
        mixed = conv_rows(lefts, weights, [own, other], row, step, cols)
        before = y1[pl.ds(row + 1, step)].reshape(step * cols, half).astype(F32)
        rounded = (before + mixed).astype(BF16).astype(F32)
        for lane in range(0, half, 128):
            spread[...] = rounded[:, lane : lane + 128]
            for r in range(step):
                for c in range(groups):
                    send[c, row + r, :, lane : lane + 128] = spread[
                        pl.ds(r * cols + c, cols // groups, stride=groups), :
                    ].astype(BF16)


def second_conv(where, y1, mine, theirs, pieces, step):
    padded_rows, cols, half = y1.shape
    rows, channels = padded_rows - 2, 2 * half
    groups, chips = cols // GRID, channels // pieces[0].shape[3]
    return pl.pallas_call(
        functools.partial(second_conv_kernel, step),
        out_shape=jax.ShapeDtypeStruct((groups, rows, GRID, half), BF16),
        in_specs=[SMEM, VMEM, VMEM, VMEM] + [ANY] * len(pieces),
        out_specs=VMEM,
        scratch_shapes=[
            pltpu.VMEM((3, 3, channels, half), BF16),
            pltpu.SemaphoreType.DMA((3 * chips,)),
            pltpu.VMEM((step * cols, 128), F32),
        ],
        compiler_params=params(40),
        cost_estimate=cost(18 * rows * cols * channels * half, 18 * channels * half),
        name="second_conv",
    )(where, y1, mine, theirs, *pieces)


def rms_round(values):
    meansq = jnp.mean(values * values, axis=-1, keepdims=True)
    return (values * lax.rsqrt(meansq + 1e-06)).astype(BF16)


def window_kernel(per, picks, y2, *refs):
    sources, outs, sems = refs[:6], refs[6:-10], refs[-1]
    (att, wide, thin), weights = refs[-10:-7], refs[-7:-1]
    out, edge = outs[0], outs[-1]
    copies = [
        pltpu.make_async_copy(source, dest, sems.at[i])
        for i, (source, dest) in enumerate(zip(sources, weights))
    ]
    for copy in copies:
        copy.start()
    w_query, w_key, w_value, w_out, w_in, w_down = weights
    grid, channels = out.shape[0], out.shape[2]
    cells = grid * GRID
    current = jnp.concatenate(
        [
            jnp.concatenate(
                [y2[:, side, :, r].reshape(cells, -1) for side in range(y2.shape[1])], axis=1
            )
            for r in range(per)
        ],
        axis=0,
    ).astype(F32)
    normed = rms_round(current)
    dot = functools.partial(jnp.dot, preferred_element_type=F32)
    for copy in copies[:3]:
        copy.wait()
    queries = (dot(normed, w_query[...]).astype(BF16) * BF16(HD**-0.5)).astype(BF16)
    keys = dot(normed, w_key[...]).astype(BF16)
    values = dot(normed, w_value[...]).astype(BF16)
    pair = 2 * HD
    low = lax.broadcasted_iota(jnp.int32, (cells, pair), 1) < HD
    zero = jnp.zeros((cells, pair), BF16)
    for r in range(per):
        for lane in range(0, channels, pair):
            spot = (slice(r * cells, (r + 1) * cells), slice(lane, lane + pair))
            query, key, value = queries[spot], keys[spot], values[spot]
            halves = []
            for keep in (jnp.where(low, query, zero), jnp.where(low, zero, query)):
                scores = lax.dot_general(
                    keep, key, (((1,), (1,)), ((), ())), preferred_element_type=F32
                )
                lifted = jnp.exp(scores - jnp.max(scores, axis=-1, keepdims=True))
                probs = lifted * (1.0 / jnp.sum(lifted, axis=-1, keepdims=True))
                halves.append(dot(probs.astype(BF16), value))
            att[spot] = jnp.where(low, halves[0], halves[1]).astype(BF16)
    for copy in copies[3:]:
        copy.wait()
    current = (current + dot(att[...], w_out[...])).astype(BF16).astype(F32)
    normed = rms_round(current)
    units = w_in.shape[1]
    lowered = None
    for start in range(0, units, channels):
        span = slice(start, start + channels)
        hidden = gelu(dot(normed, w_in[:, span])).astype(BF16)
        term = dot(hidden, w_down[span, :])
        lowered = term if lowered is None else lowered + term
    latent = (current + lowered).astype(BF16)
    wide_values = latent.astype(F32)
    for r in range(per):
        out[:, r * GRID : (r + 1) * GRID] = latent[r * cells : (r + 1) * cells].reshape(
            grid, GRID, channels
        )
    kept = grid // 2
    for lane in range(0, channels, 128):
        wide[...] = wide_values[:, lane : lane + 128]
        for d in range(picks.shape[0]):
            for r in range(per):
                first = r * cells + (grid // 4) * GRID + picks[d]
                thin[pl.ds(d * kept * per + r, kept, stride=per), :] = wide[
                    pl.ds(first, kept, stride=GRID), :
                ]
        edge[:, edge.shape[1] - kept * per :, lane : lane + 128] = (
            thin[...].astype(BF16).reshape(picks.shape[0], kept * per, 128)
        )


def windows(joined, picks, y2, w_query, w_key, w_value, w_out, w_in, w_down):
    grid, per, channels = y2.shape[0] * y2.shape[2], y2.shape[3], w_query.shape[0]
    cells, units, dests = grid * GRID, w_in.shape[1], picks.shape[0]
    total = per * cells
    kept = per * grid // 2
    flops = 2 * total * channels * (4 * channels + 2 * units + 2 * cells)
    shapes = [(grid, per * GRID, channels), (dests, kept, channels)]
    if joined:
        shapes = [(grid, per * GRID + kept, channels)]
    return pl.pallas_call(
        functools.partial(window_kernel, per),
        out_shape=tuple(jax.ShapeDtypeStruct(shape, BF16) for shape in shapes),
        in_specs=[SMEM, VMEM] + [ANY] * 6,
        out_specs=tuple(VMEM for _ in shapes),
        scratch_shapes=[
            pltpu.VMEM((total, channels), BF16),
            pltpu.VMEM((total, 128), F32),
            pltpu.VMEM((dests * kept, 128), F32),
        ]
        + [
            pltpu.VMEM(weight.shape, BF16)
            for weight in (w_query, w_key, w_value, w_out, w_in, w_down)
        ]
        + [pltpu.SemaphoreType.DMA((6,))],
        compiler_params=params(56),
        cost_estimate=cost(flops, 8 * total * channels, total * (cells * 8 + units)),
        name="windows",
    )(picks, y2, w_query, w_key, w_value, w_out, w_in, w_down)


def upsample_kernel(info, where, arrived, mine, theirs, *refs):
    ends, (out, field, weights, spread, sems) = refs[:4], refs[4:]
    taps, depth, half = mine.shape[0], mine.shape[2], mine.shape[3]
    core = info[0]
    copies = []
    for index, (source, side) in enumerate(((mine, core), (theirs, 1 - core))):
        lanes = pl.ds(pl.multiple_of(side * half, half), half)
        copies.append(pltpu.make_async_copy(source, weights.at[:, :, :, lanes], sems.at[index]))
    for copy in copies:
        copy.start()
    framed, rows, channels = field.shape
    width = framed - 2
    for j in range(framed):
        column = arrived[info[3 + j], pl.ds(arrived.shape[1] - rows, rows)]
        if j == 0:
            column = column * info[1].astype(F32).astype(BF16)
        if j == framed - 1:
            column = column * info[2].astype(F32).astype(BF16)
        field[j] = column
    for copy in copies:
        copy.wait()
    share = ends[0].shape[3]
    far = where[where.shape[0] - 4]
    depth_rows = pl.ds(pl.multiple_of(far * share, share), share)
    late = []
    for side, (pair, third) in ((core, ends[:2]), (1 - core, ends[2:])):
        lanes = pl.ds(pl.multiple_of(side * half, half), half)
        for source, tap in ((pair.at[0, 0], where[0]), (pair.at[1, 0], 1), (third.at[0, 0], 2 - where[0])):
            target = weights.at[tap, :, depth_rows, lanes]
            late.append(pltpu.make_async_copy(source, target, sems.at[2 + len(late)]))
    for copy in late:
        copy.start()
    for copy in late:
        copy.wait()
    flat = field[...].reshape(framed * rows, channels)
    size = width * rows
    place = lax.broadcasted_iota(jnp.int32, (size, 128), 0) % rows
    out_cols = 2 * width
    for start in range(0, channels, 256):
        span = slice(start, start + 256)
        columns = []
        for a in range(3):
            p0, p1, p2 = [
                jnp.dot(flat, weights[a, b, :, span], preferred_element_type=F32)
                for b in range(3)
            ]
            middle = p1[rows : rows + size]
            columns.append(
                (
                    p0[:size] + middle + p2[rows : rows + size],
                    p0[rows : rows + size] + middle + p2[2 * rows : 2 * rows + size],
                )
            )
        for lane in range(0, 256, 128):
            for dj in range(2):
                c0, c1, c2 = [columns[a][dj][:, lane : lane + 128] for a in range(3)]
                above = jnp.where(place == 0, 0.0, pltpu.roll(c0, 1, 0))
                below = jnp.where(place == rows - 1, 0.0, pltpu.roll(c2, size - 1, 0))
                for di, value in enumerate((above + c1 + c2, c0 + c1 + below)):
                    for j in range(width):
                        first = di * out_cols + 2 * j + dj
                        spread[pl.ds(first, rows, stride=2 * out_cols), :] = value[
                            j * rows : (j + 1) * rows
                        ]
            out[:, :, start + lane : start + lane + 128] = (
                spread[...].astype(BF16).reshape(2 * rows, out_cols, 128)
            )


def upsample(info, where, arrived, mine, theirs, ends, rows, width):
    channels = arrived.shape[2]
    framed = width + 2
    return pl.pallas_call(
        upsample_kernel,
        out_shape=jax.ShapeDtypeStruct((2 * rows, 2 * width, channels), BF16),
        in_specs=[SMEM, SMEM, VMEM] + [ANY] * 6,
        out_specs=VMEM,
        scratch_shapes=[
            pltpu.VMEM((framed, rows, channels), BF16),
            pltpu.VMEM((3, 3, channels, channels), BF16),
            pltpu.VMEM((4 * rows * width, 128), F32),
            pltpu.SemaphoreType.DMA((8,)),
        ],
        compiler_params=params(40),
        cost_estimate=cost(18 * framed * rows * channels * channels, 18 * channels * channels),
        name="upsample",
    )(info, where, arrived, mine, theirs, *ends)


def settle_kernel(arrived, earlier, out, spread):
    per, _, channels = out.shape
    groups = arrived.shape[0]
    cells = out.shape[1] // groups
    for r in range(per):
        for lane in range(0, channels, 128):
            for c in range(groups):
                spread[pl.ds(c, cells, stride=groups), :] = arrived[
                    c, r * cells : (r + 1) * cells, lane : lane + 128
                ].astype(F32)
            out[r, :, lane : lane + 128] = spread[...].astype(BF16)


def settle(arrived, earlier, per):
    groups, cells, channels = arrived.shape[0], GRID, arrived.shape[2]
    return pl.pallas_call(
        settle_kernel,
        out_shape=jax.ShapeDtypeStruct((per, groups * cells, channels), BF16),
        in_specs=[VMEM, ANY],
        out_specs=VMEM,
        scratch_shapes=[pltpu.VMEM((groups * cells, 128), F32)],
        compiler_params=params(8),
        name="settle",
    )(arrived, earlier)


def on_device(
    latent, conv_first, conv_second, w_query, w_key, w_value, w_out, w_in, w_down, conv_up
):
    n = lax.axis_size("row")
    chips = n // 2
    device = lax.axis_index("row")
    core, chip = device % 2, device // 2
    per, cols, channels = latent.shape
    half = channels // 2
    flip = lax.axis_index("parts") % 2 == 1
    swap = [(i, i ^ 1) for i in range(n)]

    def unit_of(share):
        mine = lax.dynamic_slice_in_dim(share, core * half, half, axis=share.ndim - 1)
        given = lax.dynamic_slice_in_dim(share, (1 - core) * half, half, axis=share.ndim - 1)
        got = lax.ppermute(given, "row", swap)
        depth = share.ndim - 2
        return jnp.where(
            core == 0,
            jnp.concatenate([mine, got], axis=depth),
            jnp.concatenate([got, mine], axis=depth),
        )

    units = unit_of(jnp.stack([conv_first, conv_second, conv_up], axis=1))
    pair, last = Gather(units[:, :2], flip, False), Gather(units[:, 2:], flip, True)
    count = chips // 2
    pair.step(1)
    latent_later, _ = lax.optimization_barrier((latent, pair.up))

    edges = []
    for i in range(chips - 1):
        edges += [(2 * i + 1, 2 * i + 2), (2 * i + 2, 2 * i + 1)]
    beside = jnp.where(core == 0, latent_later[:2], latent_later[-2:])
    near = lax.ppermute(beside, "row", edges)
    partner = lax.ppermute(latent_later, "row", swap)
    far = lax.ppermute(near, "row", swap)
    for index in range(2, count):
        if len(pair.batches) > 1:
            pair.after(pair.batches[-2])
        pair.step(index)
    since, joint = pair.sent, list(pair.batches)
    pair.cross(slice(0, 1))
    last.after(pair.up)
    last.step(1)
    pair.after((joint[-1], near))
    pair.step(count)
    pair.finals = last.before(pair.finals)
    pair.cross_final(0)
    field = jnp.where(
        core == 0,
        jnp.concatenate([near, latent, partner, far], axis=0),
        jnp.concatenate([far, partner, latent, near], axis=0),
    )
    active = gelu(field.astype(F32)).astype(BF16)
    active, pair.finals[1] = lax.optimization_barrier((active, pair.finals[1]))
    first_pieces = pair.result()
    pair.batches = joint + [pair.cross_late(1, since)]
    last.after(active)
    last.step(2)

    place = jnp.where(chip % 2 == 0, chip // 2, chips - 1 - chip // 2)
    owners = chip_at((place + jnp.array(ring_positions(chips), jnp.int32)) % chips, chips)
    top = jnp.where(chip == 0, 1, 0)
    bottom = 2 * per + 2 - jnp.where(chip == chips - 1, 1, 0)
    where = jnp.concatenate(
        [jnp.where(flip, 2, 0)[None], owners, jnp.stack([core, top, bottom])]
    ).astype(jnp.int32)

    y1, active2 = first_conv(where, active, field, first_pieces, 3)
    active2 = last.before(active2)
    active2, pair.batches = lax.optimization_barrier((active2, pair.batches))
    second_pieces = pair.result()
    theirs = lax.ppermute(active2, "row", swap)
    last.after(active2)
    for index in range(3, count):
        last.step(index)
    y2 = second_conv(where, y1, active2, theirs, second_pieces, 4)

    y2 = last.before(y2)
    groups = cols // GRID
    subs = n // groups
    index_groups = None
    if subs > 1:
        index_groups = [[k * subs + s for k in range(groups)] for s in range(subs)]
    if subs > 1:
        kept = lax.dynamic_slice_in_dim(y2, core * per, per, axis=1)
        passed = lax.dynamic_slice_in_dim(y2, (1 - core) * per, per, axis=1)
        partner = lax.ppermute(passed, "row", swap)
        y2 = jnp.where(
            core == 0,
            jnp.concatenate([kept, partner], axis=3),
            jnp.concatenate([partner, kept], axis=3),
        )
    owned = lax.all_to_all(
        y2, "row", split_axis=0, concat_axis=0, axis_index_groups=index_groups, tiled=True
    )
    up_mine = assemble(where, last.result(), chips)
    owned, _ = lax.optimization_barrier((owned, up_mine))
    up_theirs = lax.ppermute(up_mine, "row", swap)
    last.after(owned)
    last.step(count)
    sides = 2 if subs == 1 else 1
    owned = owned.reshape(GRID // 2, sides, 2, per, GRID, channels // sides)
    width = cols // 2 // n
    dests = jnp.arange(n, dtype=jnp.int32)
    starts = cols // 4 + width * dests - 1
    column = device // subs
    picks = jnp.clip((starts - column + groups - 1) // groups, 0, GRID - 1).astype(jnp.int32)
    sent = windows(subs == 1, picks, owned, w_query, w_key, w_value, w_out, w_in, w_down)

    sent = last.before(sent)
    sent, last.finals = lax.optimization_barrier((sent, last.finals))
    last.cross_final(0)
    back = lax.all_to_all(
        sent[0],
        "row",
        split_axis=0,
        concat_axis=0,
        axis_index_groups=index_groups,
        tiled=True,
    )
    central = back
    rows = subs * per * GRID // 2
    if subs > 1:
        central = lax.all_to_all(sent[1], "row", split_axis=0, concat_axis=0, tiled=True)
        central = central.reshape(groups, subs, GRID // 2, per, channels)
        central = central.transpose(0, 2, 1, 3, 4).reshape(groups, rows, channels)
    ends = [last.finals[0], last.batches[-1]]
    ends += [lax.ppermute(end, "row", swap) for end in ends]
    sources = (cols // 4 + width * device - 1 + jnp.arange(width + 2, dtype=jnp.int32)) % groups
    info = jnp.concatenate(
        [jnp.stack([core, (device > 0).astype(jnp.int32), (device < n - 1).astype(jnp.int32)]), sources]
    ).astype(jnp.int32)
    upsampled = upsample(info, where, central, up_mine, up_theirs, ends, rows, width)
    return (settle(back, upsampled, per), upsampled)


def solution(mesh):
    placed = (
        P(("parts", "row"), None, None),
        P(None, None, "row", None),
        P(None, None, "row", None),
        P(),
        P(),
        P(),
        P(),
        P(),
        P(),
        P(None, None, "row", None),
    )
    return jax.shard_map(
        on_device,
        mesh=mesh,
        in_specs=placed,
        out_specs=(P(("parts", "row"), None, None), P("parts", "row", None)),
        check_vma=False,
    )
```

```python
import functools

import jax
import jax.numpy as jnp
from jax import lax
from jax.experimental import pallas as pl
from jax.experimental.pallas import tpu as pltpu
from jax.sharding import PartitionSpec as P

HD = 64
GRID = 16
F32, BF16 = jnp.float32, jnp.bfloat16
ANY = pl.BlockSpec(memory_space=pl.ANY)
VMEM = pl.BlockSpec(memory_space=pltpu.VMEM)
SMEM = pl.BlockSpec(memory_space=pltpu.SMEM)


def gelu(x):
    return jax.nn.gelu(x, approximate=True)


def params(mib):
    return pltpu.CompilerParams(vmem_limit_bytes=mib << 20)


def cost(flops, size, transcendentals=0):
    return pl.CostEstimate(
        flops=int(flops), bytes_accessed=int(size), transcendentals=int(transcendentals)
    )


def chip_at(position, chips):
    return jnp.where(position < chips // 2, 2 * position, 2 * (chips - 1 - position) + 1)


def ring_of(chips):
    return list(range(0, chips, 2)) + list(range(1, chips, 2))[::-1]


def ring_positions(chips):
    steps = [0]
    for step in range(1, chips // 2 + 1):
        steps.append(-step)
        if step <= (chips - 1) // 2:
            steps.append(step)
    return steps


class Gather:
    def __init__(self, unit, flip, whole):
        turned = jnp.where(flip, unit[::-1], unit)
        self.chips, self.whole = lax.axis_size("row") // 2, whole
        self.up = self.down = turned[:2]
        self.rest = turned[2]
        self.pieces, self.finals, self.batches, self.sent = [self.up], [], [], 1

    def after(self, value):
        self.up, self.down, _ = lax.optimization_barrier((self.up, self.down, value))

    def before(self, value):
        held = (value, self.up, self.down, self.finals, self.batches[:-1])
        return lax.optimization_barrier(held)[0]

    def step(self, index):
        ring = ring_of(self.chips)
        forward = [
            (2 * ring[i] + core, 2 * ring[(i + 1) % self.chips] + core)
            for i in range(self.chips)
            for core in (0, 1)
        ]
        backward = [(b, a) for a, b in forward]
        across = [(i, i ^ 1) for i in range(lax.axis_size("parts"))]
        if index == self.chips // 2:
            ways = ((self.up, forward), (self.down, backward))
            for kernel in range(self.up.shape[1]):
                value, pairs = ways[kernel % 2]
                self.finals.append(lax.ppermute(value[:, kernel : kernel + 1], "row", pairs))
            return
        self.up = lax.ppermute(self.up, "row", forward)
        self.down = lax.ppermute(self.down, "row", backward)
        self.pieces += [self.up, self.down]
        near = len(self.pieces) < self.chips - 1
        if (near and len(self.pieces) - self.sent >= self.chips // 4) or (not near and self.whole):
            self.cross(slice(None))

    def cross(self, kernels):
        across = [(i, i ^ 1) for i in range(lax.axis_size("parts"))]
        thirds = [piece[0, kernels] for piece in self.pieces[self.sent :]]
        self.batches.append(lax.ppermute(jnp.stack(thirds), "parts", across))
        self.sent = len(self.pieces)

    def cross_final(self, kernel):
        across = [(i, i ^ 1) for i in range(lax.axis_size("parts"))]
        self.batches.append(lax.ppermute(self.finals[kernel][:1], "parts", across))

    def cross_late(self, kernel, since):
        across = [(i, i ^ 1) for i in range(lax.axis_size("parts"))]
        late = self.pieces[since:] + self.finals[kernel : kernel + 1]
        thirds = [piece[0, -1:] for piece in late]
        return lax.ppermute(jnp.stack(thirds), "parts", across)

    def result(self):
        return self.pieces + self.finals + [self.rest] + self.batches


def start_copies(where, refs, index, target, sems, final=True):
    chips = target.shape[2] // refs[0].shape[3]
    near, kernels = chips - 1, refs[0].shape[1] if final else 0
    finals, rest = refs[near : near + kernels], refs[near + kernels]
    batches = refs[near + kernels + 1 :]
    pieces = [piece.at[:, index] for piece in refs[:near]]
    pieces += [piece.at[:, 0] for piece in finals[index : index + 1]]
    thirds = [rest.at[index]]
    for batch in batches:
        kernel = min(index, batch.shape[1] - 1)
        thirds += [batch.at[i, kernel] for i in range(batch.shape[0])]
    first = where[0]
    share = refs[0].shape[3]
    jobs = []
    for i, piece in enumerate(pieces):
        rows = pl.ds(pl.multiple_of(where[1 + i] * share, share), share)
        jobs.append((piece.at[0], target.at[first, :, rows, :]))
        jobs.append((piece.at[1], target.at[1, :, rows, :]))
        jobs.append((thirds[i], target.at[2 - first, :, rows, :]))
    copies = [
        pltpu.make_async_copy(source, dest, sems.at[i]) for i, (source, dest) in enumerate(jobs)
    ]
    for copy in copies:
        copy.start()
    return copies


def assemble_kernel(where, *refs):
    target, sems = refs[-2:]
    for copy in start_copies(where, refs[:-2], 0, target, sems, False):
        copy.wait()


def assemble(where, pieces, chips):
    share, outs = pieces[0].shape[3:]
    shape = (3, 3, share * chips, outs)
    return pl.pallas_call(
        assemble_kernel,
        out_shape=jax.ShapeDtypeStruct(shape, BF16),
        in_specs=[SMEM] + [ANY] * len(pieces),
        out_specs=VMEM,
        scratch_shapes=[pltpu.SemaphoreType.DMA((3 * chips,))],
        compiler_params=params(12),
        cost_estimate=cost(0, 4 * 9 * share * chips * outs),
        name="assemble",
    )(where, *pieces)


def conv_rows(lefts, weights, depths, row, rows, cols):
    total = []
    for b in range(3):
        part = None
        for a in range(3):
            for left, depth in zip(lefts, depths):
                block = left(row + a, rows).reshape(rows * cols, -1)
                term = jnp.dot(block, weights[a, b, depth, :], preferred_element_type=F32)
                part = term if part is None else part + term
        total.append(part)
    size = rows * cols
    col = lax.broadcasted_iota(jnp.int32, total[0].shape, 0) % cols
    left = jnp.where(col == 0, 0.0, pltpu.roll(total[0], 1, 0))
    right = jnp.where(col == cols - 1, 0.0, pltpu.roll(total[2], size - 1, 0))
    return left + total[1] + right


def first_conv_kernel(step, where, act, lat, *refs):
    pieces, (y_out, act_out, weights, sems) = refs[:-4], refs[-4:]
    copies = start_copies(where, pieces, 0, weights, sems)
    core, top, bottom = where[where.shape[0] - 3], where[where.shape[0] - 2], where[where.shape[0] - 1]
    rows, cols, half = y_out.shape
    lanes = pl.ds(pl.multiple_of(core * half, half), half)
    for copy in copies:
        copy.wait()

    def body(i, carry):
        row = i * step
        mixed = conv_rows(
            [lambda r, k: act[pl.ds(r, k)]], weights, [slice(None)], row, step, cols
        ).reshape(step, cols, half)
        y = (lat[pl.ds(row + 1, step), :, lanes].astype(F32) + mixed).astype(BF16)
        y_out[pl.ds(row, step)] = y
        active = gelu(y.astype(F32))
        place = row + lax.broadcasted_iota(jnp.int32, active.shape, 0)
        active = jnp.where((place >= top) & (place < bottom), active, 0.0)
        act_out[pl.ds(row, step)] = active.astype(BF16)
        return carry

    lax.fori_loop(0, rows // step, body, 0)


def first_conv(where, act, lat, pieces, step):
    total_rows, cols, channels = act.shape
    rows, half, chips = total_rows - 2, channels // 2, channels // pieces[0].shape[3]
    out = jax.ShapeDtypeStruct((rows, cols, half), BF16)
    return pl.pallas_call(
        functools.partial(first_conv_kernel, step),
        out_shape=(out, out),
        in_specs=[SMEM, VMEM, VMEM] + [ANY] * len(pieces),
        out_specs=(VMEM, VMEM),
        scratch_shapes=[
            pltpu.VMEM((3, 3, channels, half), BF16),
            pltpu.SemaphoreType.DMA((3 * chips,)),
        ],
        compiler_params=params(40),
        cost_estimate=cost(
            18 * rows * cols * channels * half, 18 * channels * half, rows * cols * half
        ),
        name="first_conv",
    )(where, act, lat, *pieces)


def second_conv_kernel(step, where, y1, mine, theirs, *refs):
    pieces, (send, weights, sems, spread) = refs[:-4], refs[-4:]
    copies = start_copies(where, pieces, 1, weights, sems)
    core = where[where.shape[0] - 3]
    groups, rows, _, half = send.shape
    cols = mine.shape[1]
    own = pl.ds(pl.multiple_of(core * half, half), half)
    other = pl.ds(pl.multiple_of((1 - core) * half, half), half)
    for copy in copies:
        copy.wait()
    lefts = [lambda r, k: mine[pl.ds(r, k)], lambda r, k: theirs[pl.ds(r, k)]]
    for row in range(0, rows, step):
        mixed = conv_rows(lefts, weights, [own, other], row, step, cols)
        before = y1[pl.ds(row + 1, step)].reshape(step * cols, half).astype(F32)
        rounded = (before + mixed).astype(BF16).astype(F32)
        for lane in range(0, half, 128):
            spread[...] = rounded[:, lane : lane + 128]
            for r in range(step):
                for c in range(groups):
                    send[c, row + r, :, lane : lane + 128] = spread[
                        pl.ds(r * cols + c, cols // groups, stride=groups), :
                    ].astype(BF16)


def second_conv(where, y1, mine, theirs, pieces, step):
    padded_rows, cols, half = y1.shape
    rows, channels = padded_rows - 2, 2 * half
    groups, chips = cols // GRID, channels // pieces[0].shape[3]
    return pl.pallas_call(
        functools.partial(second_conv_kernel, step),
        out_shape=jax.ShapeDtypeStruct((groups, rows, GRID, half), BF16),
        in_specs=[SMEM, VMEM, VMEM, VMEM] + [ANY] * len(pieces),
        out_specs=VMEM,
        scratch_shapes=[
            pltpu.VMEM((3, 3, channels, half), BF16),
            pltpu.SemaphoreType.DMA((3 * chips,)),
            pltpu.VMEM((step * cols, 128), F32),
        ],
        compiler_params=params(40),
        cost_estimate=cost(18 * rows * cols * channels * half, 18 * channels * half),
        name="second_conv",
    )(where, y1, mine, theirs, *pieces)


def rms_round(values):
    meansq = jnp.mean(values * values, axis=-1, keepdims=True)
    return (values * lax.rsqrt(meansq + 1e-06)).astype(BF16)


def window_kernel(per, picks, y2, *refs):
    sources, outs, sems = refs[:6], refs[6:-10], refs[-1]
    (att, wide, thin), weights = refs[-10:-7], refs[-7:-1]
    out, edge = outs[0], outs[-1]
    copies = [
        pltpu.make_async_copy(source, dest, sems.at[i])
        for i, (source, dest) in enumerate(zip(sources, weights))
    ]
    for copy in copies:
        copy.start()
    w_query, w_key, w_value, w_out, w_in, w_down = weights
    grid, channels = out.shape[0], out.shape[2]
    cells = grid * GRID
    current = jnp.concatenate(
        [
            jnp.concatenate(
                [y2[:, side, :, r].reshape(cells, -1) for side in range(y2.shape[1])], axis=1
            )
            for r in range(per)
        ],
        axis=0,
    ).astype(F32)
    normed = rms_round(current)
    dot = functools.partial(jnp.dot, preferred_element_type=F32)
    for copy in copies[:3]:
        copy.wait()
    queries = (dot(normed, w_query[...]).astype(BF16) * BF16(HD**-0.5)).astype(BF16)
    keys = dot(normed, w_key[...]).astype(BF16)
    values = dot(normed, w_value[...]).astype(BF16)
    pair = 2 * HD
    low = lax.broadcasted_iota(jnp.int32, (cells, pair), 1) < HD
    zero = jnp.zeros((cells, pair), BF16)
    for r in range(per):
        for lane in range(0, channels, pair):
            spot = (slice(r * cells, (r + 1) * cells), slice(lane, lane + pair))
            query, key, value = queries[spot], keys[spot], values[spot]
            halves = []
            for keep in (jnp.where(low, query, zero), jnp.where(low, zero, query)):
                scores = lax.dot_general(
                    keep, key, (((1,), (1,)), ((), ())), preferred_element_type=F32
                )
                lifted = jnp.exp(scores - jnp.max(scores, axis=-1, keepdims=True))
                probs = lifted * (1.0 / jnp.sum(lifted, axis=-1, keepdims=True))
                halves.append(dot(probs.astype(BF16), value))
            att[spot] = jnp.where(low, halves[0], halves[1]).astype(BF16)
    for copy in copies[3:]:
        copy.wait()
    current = (current + dot(att[...], w_out[...])).astype(BF16).astype(F32)
    normed = rms_round(current)
    units = w_in.shape[1]
    lowered = None
    for start in range(0, units, channels):
        span = slice(start, start + channels)
        hidden = gelu(dot(normed, w_in[:, span])).astype(BF16)
        term = dot(hidden, w_down[span, :])
        lowered = term if lowered is None else lowered + term
    latent = (current + lowered).astype(BF16)
    wide_values = latent.astype(F32)
    for r in range(per):
        out[:, r * GRID : (r + 1) * GRID] = latent[r * cells : (r + 1) * cells].reshape(
            grid, GRID, channels
        )
    kept = grid // 2
    for lane in range(0, channels, 128):
        wide[...] = wide_values[:, lane : lane + 128]
        for d in range(picks.shape[0]):
            for r in range(per):
                first = r * cells + (grid // 4) * GRID + picks[d]
                thin[pl.ds(d * kept * per + r, kept, stride=per), :] = wide[
                    pl.ds(first, kept, stride=GRID), :
                ]
        edge[:, edge.shape[1] - kept * per :, lane : lane + 128] = (
            thin[...].astype(BF16).reshape(picks.shape[0], kept * per, 128)
        )


def windows(joined, picks, y2, w_query, w_key, w_value, w_out, w_in, w_down):
    grid, per, channels = y2.shape[0] * y2.shape[2], y2.shape[3], w_query.shape[0]
    cells, units, dests = grid * GRID, w_in.shape[1], picks.shape[0]
    total = per * cells
    kept = per * grid // 2
    flops = 2 * total * channels * (4 * channels + 2 * units + 2 * cells)
    shapes = [(grid, per * GRID, channels), (dests, kept, channels)]
    if joined:
        shapes = [(grid, per * GRID + kept, channels)]
    return pl.pallas_call(
        functools.partial(window_kernel, per),
        out_shape=tuple(jax.ShapeDtypeStruct(shape, BF16) for shape in shapes),
        in_specs=[SMEM, VMEM] + [ANY] * 6,
        out_specs=tuple(VMEM for _ in shapes),
        scratch_shapes=[
            pltpu.VMEM((total, channels), BF16),
            pltpu.VMEM((total, 128), F32),
            pltpu.VMEM((dests * kept, 128), F32),
        ]
        + [
            pltpu.VMEM(weight.shape, BF16)
            for weight in (w_query, w_key, w_value, w_out, w_in, w_down)
        ]
        + [pltpu.SemaphoreType.DMA((6,))],
        compiler_params=params(56),
        cost_estimate=cost(flops, 8 * total * channels, total * (cells * 8 + units)),
        name="windows",
    )(picks, y2, w_query, w_key, w_value, w_out, w_in, w_down)


def upsample_kernel(info, where, arrived, mine, theirs, *refs):
    ends, outs, (lines, field, weights, spread, sems) = refs[:4], refs[4:-5], refs[-5:]
    out = outs[0]
    taps, depth, half = mine.shape[0], mine.shape[2], mine.shape[3]
    core = info[0]
    copies = []
    for index, (source, side) in enumerate(((mine, core), (theirs, 1 - core))):
        lanes = pl.ds(pl.multiple_of(side * half, half), half)
        copies.append(pltpu.make_async_copy(source, weights.at[:, :, :, lanes], sems.at[index]))
    for copy in copies:
        copy.start()
    framed, rows, channels = field.shape
    width = framed - 2
    for settled in outs[1:]:
        settle_kernel(arrived, None, settled, lines)
    for j in range(framed):
        column = arrived[info[3 + j], pl.ds(arrived.shape[1] - rows, rows)]
        if j == 0:
            column = column * info[1].astype(F32).astype(BF16)
        if j == framed - 1:
            column = column * info[2].astype(F32).astype(BF16)
        field[j] = column
    for copy in copies:
        copy.wait()
    share = ends[0].shape[3]
    far = where[where.shape[0] - 4]
    depth_rows = pl.ds(pl.multiple_of(far * share, share), share)
    late = []
    for side, (pair, third) in ((core, ends[:2]), (1 - core, ends[2:])):
        lanes = pl.ds(pl.multiple_of(side * half, half), half)
        for source, tap in ((pair.at[0, 0], where[0]), (pair.at[1, 0], 1), (third.at[0, 0], 2 - where[0])):
            target = weights.at[tap, :, depth_rows, lanes]
            late.append(pltpu.make_async_copy(source, target, sems.at[2 + len(late)]))
    for copy in late:
        copy.start()
    for copy in late:
        copy.wait()
    flat = field[...].reshape(framed * rows, channels)
    size = width * rows
    place = lax.broadcasted_iota(jnp.int32, (size, 128), 0) % rows
    out_cols = 2 * width
    for start in range(0, channels, 256):
        span = slice(start, start + 256)
        columns = []
        for a in range(3):
            p0, p1, p2 = [
                jnp.dot(flat, weights[a, b, :, span], preferred_element_type=F32)
                for b in range(3)
            ]
            middle = p1[rows : rows + size]
            columns.append(
                (
                    p0[:size] + middle + p2[rows : rows + size],
                    p0[rows : rows + size] + middle + p2[2 * rows : 2 * rows + size],
                )
            )
        for lane in range(0, 256, 128):
            for dj in range(2):
                c0, c1, c2 = [columns[a][dj][:, lane : lane + 128] for a in range(3)]
                above = jnp.where(place == 0, 0.0, pltpu.roll(c0, 1, 0))
                below = jnp.where(place == rows - 1, 0.0, pltpu.roll(c2, size - 1, 0))
                for di, value in enumerate((above + c1 + c2, c0 + c1 + below)):
                    for j in range(width):
                        first = di * out_cols + 2 * j + dj
                        spread[pl.ds(first, rows, stride=2 * out_cols), :] = value[
                            j * rows : (j + 1) * rows
                        ]
            out[:, :, start + lane : start + lane + 128] = (
                spread[...].astype(BF16).reshape(2 * rows, out_cols, 128)
            )


def upsample(info, where, arrived, mine, theirs, ends, rows, width, per):
    channels = arrived.shape[2]
    framed, line = width + 2, arrived.shape[0] * GRID
    shapes = [(2 * rows, 2 * width, channels)]
    if arrived.shape[1] > rows:
        shapes.append((per, line, channels))
    return pl.pallas_call(
        upsample_kernel,
        out_shape=tuple(jax.ShapeDtypeStruct(shape, BF16) for shape in shapes),
        in_specs=[SMEM, SMEM, VMEM] + [ANY] * 6,
        out_specs=tuple(VMEM for _ in shapes),
        scratch_shapes=[
            pltpu.VMEM((line, 128), F32),
            pltpu.VMEM((framed, rows, channels), BF16),
            pltpu.VMEM((3, 3, channels, channels), BF16),
            pltpu.VMEM((4 * rows * width, 128), F32),
            pltpu.SemaphoreType.DMA((8,)),
        ],
        compiler_params=params(40),
        cost_estimate=cost(18 * framed * rows * channels * channels, 18 * channels * channels),
        name="upsample",
    )(info, where, arrived, mine, theirs, *ends)


def settle_kernel(arrived, earlier, out, spread):
    per, _, channels = out.shape
    groups = arrived.shape[0]
    cells = out.shape[1] // groups
    for r in range(per):
        for lane in range(0, channels, 128):
            for c in range(groups):
                spread[pl.ds(c, cells, stride=groups), :] = arrived[
                    c, r * cells : (r + 1) * cells, lane : lane + 128
                ].astype(F32)
            out[r, :, lane : lane + 128] = spread[...].astype(BF16)


def settle(arrived, earlier, per):
    groups, cells, channels = arrived.shape[0], GRID, arrived.shape[2]
    return pl.pallas_call(
        settle_kernel,
        out_shape=jax.ShapeDtypeStruct((per, groups * cells, channels), BF16),
        in_specs=[VMEM, ANY],
        out_specs=VMEM,
        scratch_shapes=[pltpu.VMEM((groups * cells, 128), F32)],
        compiler_params=params(8),
        name="settle",
    )(arrived, earlier)


def on_device(
    latent, conv_first, conv_second, w_query, w_key, w_value, w_out, w_in, w_down, conv_up
):
    n = lax.axis_size("row")
    chips = n // 2
    device = lax.axis_index("row")
    core, chip = device % 2, device // 2
    per, cols, channels = latent.shape
    half = channels // 2
    flip = lax.axis_index("parts") % 2 == 1
    swap = [(i, i ^ 1) for i in range(n)]

    def unit_of(share):
        mine = lax.dynamic_slice_in_dim(share, core * half, half, axis=share.ndim - 1)
        given = lax.dynamic_slice_in_dim(share, (1 - core) * half, half, axis=share.ndim - 1)
        got = lax.ppermute(given, "row", swap)
        depth = share.ndim - 2
        return jnp.where(
            core == 0,
            jnp.concatenate([mine, got], axis=depth),
            jnp.concatenate([got, mine], axis=depth),
        )

    units = unit_of(jnp.stack([conv_first, conv_second, conv_up], axis=1))
    pair, last = Gather(units[:, :2], flip, False), Gather(units[:, 2:], flip, True)
    count = chips // 2
    pair.step(1)
    latent_later, _ = lax.optimization_barrier((latent, pair.up))

    edges = []
    for i in range(chips - 1):
        edges += [(2 * i + 1, 2 * i + 2), (2 * i + 2, 2 * i + 1)]
    beside = jnp.where(core == 0, latent_later[:2], latent_later[-2:])
    near = lax.ppermute(beside, "row", edges)
    partner = lax.ppermute(latent_later, "row", swap)
    far = lax.ppermute(near, "row", swap)
    for index in range(2, count):
        if len(pair.batches) > 1:
            pair.after(pair.batches[-2])
        pair.step(index)
    since, joint = pair.sent, list(pair.batches)
    pair.cross(slice(0, 1))
    last.after(pair.up)
    last.step(1)
    pair.after((joint[-1], near, partner))
    pair.step(count)
    pair.finals = last.before(pair.finals)
    pair.cross_final(0)
    field = jnp.where(
        core == 0,
        jnp.concatenate([near, latent, partner, far], axis=0),
        jnp.concatenate([far, partner, latent, near], axis=0),
    )
    active = gelu(field.astype(F32)).astype(BF16)
    active, pair.finals[1] = lax.optimization_barrier((active, pair.finals[1]))
    first_pieces = pair.result()
    pair.batches = joint + [pair.cross_late(1, since)]
    last.after(active)
    last.step(2)

    place = jnp.where(chip % 2 == 0, chip // 2, chips - 1 - chip // 2)
    owners = chip_at((place + jnp.array(ring_positions(chips), jnp.int32)) % chips, chips)
    top = jnp.where(chip == 0, 1, 0)
    bottom = 2 * per + 2 - jnp.where(chip == chips - 1, 1, 0)
    where = jnp.concatenate(
        [jnp.where(flip, 2, 0)[None], owners, jnp.stack([core, top, bottom])]
    ).astype(jnp.int32)

    y1, active2 = first_conv(where, active, field, first_pieces, 3)
    active2 = last.before(active2)
    active2, pair.batches = lax.optimization_barrier((active2, pair.batches))
    second_pieces = pair.result()
    theirs = lax.ppermute(active2, "row", swap)
    last.after(active2)
    for index in range(3, count):
        last.step(index)
    y2 = second_conv(where, y1, active2, theirs, second_pieces, 4)

    y2 = last.before(y2)
    groups = cols // GRID
    subs = n // groups
    index_groups = None
    if subs > 1:
        index_groups = [[k * subs + s for k in range(groups)] for s in range(subs)]
    if subs > 1:
        kept = lax.dynamic_slice_in_dim(y2, core * per, per, axis=1)
        passed = lax.dynamic_slice_in_dim(y2, (1 - core) * per, per, axis=1)
        partner = lax.ppermute(passed, "row", swap)
        y2 = jnp.where(
            core == 0,
            jnp.concatenate([kept, partner], axis=3),
            jnp.concatenate([partner, kept], axis=3),
        )
    owned = lax.all_to_all(
        y2, "row", split_axis=0, concat_axis=0, axis_index_groups=index_groups, tiled=True
    )
    up_mine = assemble(where, last.result(), chips)
    owned, _ = lax.optimization_barrier((owned, up_mine))
    up_theirs = lax.ppermute(up_mine, "row", swap)
    last.after(owned)
    last.step(count)
    sides = 2 if subs == 1 else 1
    owned = owned.reshape(GRID // 2, sides, 2, per, GRID, channels // sides)
    width = cols // 2 // n
    dests = jnp.arange(n, dtype=jnp.int32)
    starts = cols // 4 + width * dests - 1
    column = device // subs
    picks = jnp.clip((starts - column + groups - 1) // groups, 0, GRID - 1).astype(jnp.int32)
    sent = windows(subs == 1, picks, owned, w_query, w_key, w_value, w_out, w_in, w_down)

    sent = last.before(sent)
    sent, last.finals = lax.optimization_barrier((sent, last.finals))
    last.cross_final(0)
    back = lax.all_to_all(
        sent[0],
        "row",
        split_axis=0,
        concat_axis=0,
        axis_index_groups=index_groups,
        tiled=True,
    )
    central = back
    rows = subs * per * GRID // 2
    if subs > 1:
        central = lax.all_to_all(sent[1], "row", split_axis=0, concat_axis=0, tiled=True)
        central = central.reshape(groups, subs, GRID // 2, per, channels)
        central = central.transpose(0, 2, 1, 3, 4).reshape(groups, rows, channels)
    ends = [last.finals[0], last.batches[-1]]
    ends += [lax.ppermute(end, "row", swap) for end in ends]
    sources = (cols // 4 + width * device - 1 + jnp.arange(width + 2, dtype=jnp.int32)) % groups
    info = jnp.concatenate(
        [jnp.stack([core, (device > 0).astype(jnp.int32), (device < n - 1).astype(jnp.int32)]), sources]
    ).astype(jnp.int32)
    upsampled, *settled = upsample(
        info, where, central, up_mine, up_theirs, ends, rows, width, per
    )
    latent_out = settled[0] if settled else settle(back, upsampled, per)
    return (latent_out, upsampled)


def solution(mesh):
    placed = (
        P(("parts", "row"), None, None),
        P(None, None, "row", None),
        P(None, None, "row", None),
        P(),
        P(),
        P(),
        P(),
        P(),
        P(),
        P(None, None, "row", None),
    )
    return jax.shard_map(
        on_device,
        mesh=mesh,
        in_specs=placed,
        out_specs=(P(("parts", "row"), None, None), P("parts", "row", None)),
        check_vma=False,
    )
```

```python
import functools

import jax
import jax.numpy as jnp
from jax import lax
from jax.experimental import pallas as pl
from jax.experimental.pallas import tpu as pltpu
from jax.sharding import PartitionSpec as P

HD = 64
GRID = 16
F32, BF16 = jnp.float32, jnp.bfloat16
ANY = pl.BlockSpec(memory_space=pl.ANY)
VMEM = pl.BlockSpec(memory_space=pltpu.VMEM)
SMEM = pl.BlockSpec(memory_space=pltpu.SMEM)


def gelu(x):
    return jax.nn.gelu(x, approximate=True)


def params(mib):
    return pltpu.CompilerParams(vmem_limit_bytes=mib << 20)


def cost(flops, size, transcendentals=0):
    return pl.CostEstimate(
        flops=int(flops), bytes_accessed=int(size), transcendentals=int(transcendentals)
    )


def chip_at(position, chips):
    return jnp.where(position < chips // 2, 2 * position, 2 * (chips - 1 - position) + 1)


def ring_of(chips):
    return list(range(0, chips, 2)) + list(range(1, chips, 2))[::-1]


def ring_positions(chips):
    steps = [0]
    for step in range(1, chips // 2 + 1):
        steps.append(-step)
        if step <= (chips - 1) // 2:
            steps.append(step)
    return steps


class Gather:
    def __init__(self, unit, flip, whole):
        turned = jnp.where(flip, unit[::-1], unit)
        self.chips, self.whole = lax.axis_size("row") // 2, whole
        self.up = self.down = turned[:2]
        self.rest = turned[2]
        self.pieces, self.finals, self.batches, self.sent = [self.up], [], [], 1

    def after(self, value):
        self.up, self.down, _ = lax.optimization_barrier((self.up, self.down, value))

    def before(self, value):
        held = (value, self.up, self.down, self.finals, self.batches[:-1])
        return lax.optimization_barrier(held)[0]

    def step(self, index):
        ring = ring_of(self.chips)
        forward = [
            (2 * ring[i] + core, 2 * ring[(i + 1) % self.chips] + core)
            for i in range(self.chips)
            for core in (0, 1)
        ]
        backward = [(b, a) for a, b in forward]
        across = [(i, i ^ 1) for i in range(lax.axis_size("parts"))]
        if index == self.chips // 2:
            ways = ((self.up, forward), (self.down, backward))
            for kernel in range(self.up.shape[1]):
                value, pairs = ways[kernel % 2]
                self.finals.append(lax.ppermute(value[:, kernel : kernel + 1], "row", pairs))
            return
        self.up = lax.ppermute(self.up, "row", forward)
        self.down = lax.ppermute(self.down, "row", backward)
        self.pieces += [self.up, self.down]
        near = len(self.pieces) < self.chips - 1
        if (near and len(self.pieces) - self.sent >= self.chips // 4) or (not near and self.whole):
            self.cross(slice(None))

    def cross(self, kernels):
        across = [(i, i ^ 1) for i in range(lax.axis_size("parts"))]
        thirds = [piece[0, kernels] for piece in self.pieces[self.sent :]]
        self.batches.append(lax.ppermute(jnp.stack(thirds), "parts", across))
        self.sent = len(self.pieces)

    def cross_final(self, kernel):
        across = [(i, i ^ 1) for i in range(lax.axis_size("parts"))]
        self.batches.append(lax.ppermute(self.finals[kernel][:1], "parts", across))

    def cross_late(self, kernel, since):
        across = [(i, i ^ 1) for i in range(lax.axis_size("parts"))]
        late = self.pieces[since:] + self.finals[kernel : kernel + 1]
        thirds = [piece[0, -1:] for piece in late]
        return lax.ppermute(jnp.stack(thirds), "parts", across)

    def result(self):
        return self.pieces + self.finals + [self.rest] + self.batches


def start_copies(where, refs, index, target, sems, final=True):
    chips = target.shape[2] // refs[0].shape[3]
    near, kernels = chips - 1, refs[0].shape[1] if final else 0
    finals, rest = refs[near : near + kernels], refs[near + kernels]
    batches = refs[near + kernels + 1 :]
    pieces = [piece.at[:, index] for piece in refs[:near]]
    pieces += [piece.at[:, 0] for piece in finals[index : index + 1]]
    thirds = [rest.at[index]]
    for batch in batches:
        kernel = min(index, batch.shape[1] - 1)
        thirds += [batch.at[i, kernel] for i in range(batch.shape[0])]
    first = where[0]
    share = refs[0].shape[3]
    jobs = []
    for i, piece in enumerate(pieces):
        rows = pl.ds(pl.multiple_of(where[1 + i] * share, share), share)
        jobs.append((piece.at[0], target.at[first, :, rows, :]))
        jobs.append((piece.at[1], target.at[1, :, rows, :]))
        jobs.append((thirds[i], target.at[2 - first, :, rows, :]))
    copies = [
        pltpu.make_async_copy(source, dest, sems.at[i]) for i, (source, dest) in enumerate(jobs)
    ]
    for copy in copies:
        copy.start()
    return copies


def assemble_kernel(where, *refs):
    target, sems = refs[-2:]
    for copy in start_copies(where, refs[:-2], 0, target, sems, False):
        copy.wait()


def assemble(where, pieces, chips):
    share, outs = pieces[0].shape[3:]
    shape = (3, 3, share * chips, outs)
    return pl.pallas_call(
        assemble_kernel,
        out_shape=jax.ShapeDtypeStruct(shape, BF16),
        in_specs=[SMEM] + [ANY] * len(pieces),
        out_specs=VMEM,
        scratch_shapes=[pltpu.SemaphoreType.DMA((3 * chips,))],
        compiler_params=params(12),
        cost_estimate=cost(0, 4 * 9 * share * chips * outs),
        name="assemble",
    )(where, *pieces)


def conv_rows(lefts, weights, depths, row, rows, cols):
    total = []
    for b in range(3):
        part = None
        for a in range(3):
            for left, depth in zip(lefts, depths):
                block = left(row + a, rows).reshape(rows * cols, -1)
                term = jnp.dot(block, weights[a, b, depth, :], preferred_element_type=F32)
                part = term if part is None else part + term
        total.append(part)
    size = rows * cols
    col = lax.broadcasted_iota(jnp.int32, total[0].shape, 0) % cols
    left = jnp.where(col == 0, 0.0, pltpu.roll(total[0], 1, 0))
    right = jnp.where(col == cols - 1, 0.0, pltpu.roll(total[2], size - 1, 0))
    return left + total[1] + right


def first_conv_kernel(step, where, act, lat, *refs):
    pieces, (y_out, act_out, weights, sems) = refs[:-4], refs[-4:]
    copies = start_copies(where, pieces, 0, weights, sems)
    core, top, bottom = where[where.shape[0] - 3], where[where.shape[0] - 2], where[where.shape[0] - 1]
    rows, cols, half = y_out.shape
    lanes = pl.ds(pl.multiple_of(core * half, half), half)
    for copy in copies:
        copy.wait()

    def body(i, carry):
        row = i * step
        mixed = conv_rows(
            [lambda r, k: act[pl.ds(r, k)]], weights, [slice(None)], row, step, cols
        ).reshape(step, cols, half)
        y = (lat[pl.ds(row + 1, step), :, lanes].astype(F32) + mixed).astype(BF16)
        y_out[pl.ds(row, step)] = y
        active = gelu(y.astype(F32))
        place = row + lax.broadcasted_iota(jnp.int32, active.shape, 0)
        active = jnp.where((place >= top) & (place < bottom), active, 0.0)
        act_out[pl.ds(row, step)] = active.astype(BF16)
        return carry

    lax.fori_loop(0, rows // step, body, 0)


def first_conv(where, act, lat, pieces, step):
    total_rows, cols, channels = act.shape
    rows, half, chips = total_rows - 2, channels // 2, channels // pieces[0].shape[3]
    out = jax.ShapeDtypeStruct((rows, cols, half), BF16)
    return pl.pallas_call(
        functools.partial(first_conv_kernel, step),
        out_shape=(out, out),
        in_specs=[SMEM, VMEM, VMEM] + [ANY] * len(pieces),
        out_specs=(VMEM, VMEM),
        scratch_shapes=[
            pltpu.VMEM((3, 3, channels, half), BF16),
            pltpu.SemaphoreType.DMA((3 * chips,)),
        ],
        compiler_params=params(40),
        cost_estimate=cost(
            18 * rows * cols * channels * half, 18 * channels * half, rows * cols * half
        ),
        name="first_conv",
    )(where, act, lat, *pieces)


def second_conv_kernel(step, where, y1, mine, theirs, *refs):
    pieces, (send, weights, sems, spread) = refs[:-4], refs[-4:]
    copies = start_copies(where, pieces, 1, weights, sems)
    core = where[where.shape[0] - 3]
    groups, rows, _, half = send.shape
    cols = mine.shape[1]
    own = pl.ds(pl.multiple_of(core * half, half), half)
    other = pl.ds(pl.multiple_of((1 - core) * half, half), half)
    for copy in copies:
        copy.wait()
    lefts = [lambda r, k: mine[pl.ds(r, k)], lambda r, k: theirs[pl.ds(r, k)]]
    for row in range(0, rows, step):
        mixed = conv_rows(lefts, weights, [own, other], row, step, cols)
        before = y1[pl.ds(row + 1, step)].reshape(step * cols, half).astype(F32)
        rounded = (before + mixed).astype(BF16).astype(F32)
        for lane in range(0, half, 128):
            spread[...] = rounded[:, lane : lane + 128]
            for r in range(step):
                for c in range(groups):
                    send[c, row + r, :, lane : lane + 128] = spread[
                        pl.ds(r * cols + c, cols // groups, stride=groups), :
                    ].astype(BF16)


def second_conv(where, y1, mine, theirs, pieces, step):
    padded_rows, cols, half = y1.shape
    rows, channels = padded_rows - 2, 2 * half
    groups, chips = cols // GRID, channels // pieces[0].shape[3]
    return pl.pallas_call(
        functools.partial(second_conv_kernel, step),
        out_shape=jax.ShapeDtypeStruct((groups, rows, GRID, half), BF16),
        in_specs=[SMEM, VMEM, VMEM, VMEM] + [ANY] * len(pieces),
        out_specs=VMEM,
        scratch_shapes=[
            pltpu.VMEM((3, 3, channels, half), BF16),
            pltpu.SemaphoreType.DMA((3 * chips,)),
            pltpu.VMEM((step * cols, 128), F32),
        ],
        compiler_params=params(40),
        cost_estimate=cost(18 * rows * cols * channels * half, 18 * channels * half),
        name="second_conv",
    )(where, y1, mine, theirs, *pieces)


def rms_round(values):
    meansq = jnp.mean(values * values, axis=-1, keepdims=True)
    return (values * lax.rsqrt(meansq + 1e-06)).astype(BF16)


def window_kernel(per, picks, y2, *refs):
    sources, outs, sems = refs[:6], refs[6:-10], refs[-1]
    (att, wide, thin), weights = refs[-10:-7], refs[-7:-1]
    out, edge = outs[0], outs[-1]
    copies = [
        pltpu.make_async_copy(source, dest, sems.at[i])
        for i, (source, dest) in enumerate(zip(sources, weights))
    ]
    for copy in copies:
        copy.start()
    w_query, w_key, w_value, w_out, w_in, w_down = weights
    grid, channels = out.shape[0], out.shape[2]
    cells = grid * GRID
    current = jnp.concatenate(
        [
            jnp.concatenate(
                [y2[:, side, :, r].reshape(cells, -1) for side in range(y2.shape[1])], axis=1
            )
            for r in range(per)
        ],
        axis=0,
    ).astype(F32)
    normed = rms_round(current)
    dot = functools.partial(jnp.dot, preferred_element_type=F32)
    for copy in copies[:3]:
        copy.wait()
    queries = (dot(normed, w_query[...]).astype(BF16) * BF16(HD**-0.5)).astype(BF16)
    keys = dot(normed, w_key[...]).astype(BF16)
    values = dot(normed, w_value[...]).astype(BF16)
    pair = 2 * HD
    low = lax.broadcasted_iota(jnp.int32, (cells, pair), 1) < HD
    zero = jnp.zeros((cells, pair), BF16)
    for r in range(per):
        for lane in range(0, channels, pair):
            spot = (slice(r * cells, (r + 1) * cells), slice(lane, lane + pair))
            query, key, value = queries[spot], keys[spot], values[spot]
            halves = []
            for keep in (jnp.where(low, query, zero), jnp.where(low, zero, query)):
                scores = lax.dot_general(
                    keep, key, (((1,), (1,)), ((), ())), preferred_element_type=F32
                )
                lifted = jnp.exp(scores - jnp.max(scores, axis=-1, keepdims=True))
                share = 1.0 / jnp.sum(lifted, axis=-1, keepdims=True)
                halves.append(dot(lifted.astype(BF16), value) * share)
            att[spot] = jnp.where(low, halves[0], halves[1]).astype(BF16)
    for copy in copies[3:]:
        copy.wait()
    current = (current + dot(att[...], w_out[...])).astype(BF16).astype(F32)
    normed = rms_round(current)
    units = w_in.shape[1]
    lowered = None
    for start in range(0, units, channels):
        span = slice(start, start + channels)
        hidden = gelu(dot(normed, w_in[:, span])).astype(BF16)
        term = dot(hidden, w_down[span, :])
        lowered = term if lowered is None else lowered + term
    latent = (current + lowered).astype(BF16)
    wide_values = latent.astype(F32)
    for r in range(per):
        out[:, r * GRID : (r + 1) * GRID] = latent[r * cells : (r + 1) * cells].reshape(
            grid, GRID, channels
        )
    kept = grid // 2
    for lane in range(0, channels, 128):
        wide[...] = wide_values[:, lane : lane + 128]
        for d in range(picks.shape[0]):
            for r in range(per):
                first = r * cells + (grid // 4) * GRID + picks[d]
                thin[pl.ds(d * kept * per + r, kept, stride=per), :] = wide[
                    pl.ds(first, kept, stride=GRID), :
                ]
        edge[:, edge.shape[1] - kept * per :, lane : lane + 128] = (
            thin[...].astype(BF16).reshape(picks.shape[0], kept * per, 128)
        )


def windows(joined, picks, y2, w_query, w_key, w_value, w_out, w_in, w_down):
    grid, per, channels = y2.shape[0] * y2.shape[2], y2.shape[3], w_query.shape[0]
    cells, units, dests = grid * GRID, w_in.shape[1], picks.shape[0]
    total = per * cells
    kept = per * grid // 2
    flops = 2 * total * channels * (4 * channels + 2 * units + 2 * cells)
    shapes = [(grid, per * GRID, channels), (dests, kept, channels)]
    if joined:
        shapes = [(grid, per * GRID + kept, channels)]
    return pl.pallas_call(
        functools.partial(window_kernel, per),
        out_shape=tuple(jax.ShapeDtypeStruct(shape, BF16) for shape in shapes),
        in_specs=[SMEM, VMEM] + [ANY] * 6,
        out_specs=tuple(VMEM for _ in shapes),
        scratch_shapes=[
            pltpu.VMEM((total, channels), BF16),
            pltpu.VMEM((total, 128), F32),
            pltpu.VMEM((dests * kept, 128), F32),
        ]
        + [
            pltpu.VMEM(weight.shape, BF16)
            for weight in (w_query, w_key, w_value, w_out, w_in, w_down)
        ]
        + [pltpu.SemaphoreType.DMA((6,))],
        compiler_params=params(56),
        cost_estimate=cost(flops, 8 * total * channels, total * (cells * 8 + units)),
        name="windows",
    )(picks, y2, w_query, w_key, w_value, w_out, w_in, w_down)


def upsample_kernel(info, where, arrived, mine, theirs, *refs):
    ends, outs, (lines, field, weights, spread, sems) = refs[:4], refs[4:-5], refs[-5:]
    out = outs[0]
    taps, depth, half = mine.shape[0], mine.shape[2], mine.shape[3]
    core = info[0]
    copies = []
    for index, (source, side) in enumerate(((mine, core), (theirs, 1 - core))):
        lanes = pl.ds(pl.multiple_of(side * half, half), half)
        copies.append(pltpu.make_async_copy(source, weights.at[:, :, :, lanes], sems.at[index]))
    for copy in copies:
        copy.start()
    framed, rows, channels = field.shape
    width = framed - 2
    for settled in outs[1:]:
        settle_kernel(arrived, None, settled, lines)
    for j in range(framed):
        column = arrived[info[3 + j], pl.ds(arrived.shape[1] - rows, rows)]
        if j == 0:
            column = column * info[1].astype(F32).astype(BF16)
        if j == framed - 1:
            column = column * info[2].astype(F32).astype(BF16)
        field[j] = column
    for copy in copies:
        copy.wait()
    share = ends[0].shape[3]
    far = where[where.shape[0] - 4]
    depth_rows = pl.ds(pl.multiple_of(far * share, share), share)
    late = []
    for side, (pair, third) in ((core, ends[:2]), (1 - core, ends[2:])):
        lanes = pl.ds(pl.multiple_of(side * half, half), half)
        for source, tap in ((pair.at[0, 0], where[0]), (pair.at[1, 0], 1), (third.at[0, 0], 2 - where[0])):
            target = weights.at[tap, :, depth_rows, lanes]
            late.append(pltpu.make_async_copy(source, target, sems.at[2 + len(late)]))
    for copy in late:
        copy.start()
    for copy in late:
        copy.wait()
    flat = field[...].reshape(framed * rows, channels)
    size = width * rows
    place = lax.broadcasted_iota(jnp.int32, (size, 128), 0) % rows
    out_cols = 2 * width
    for start in range(0, channels, 256):
        span = slice(start, start + 256)
        columns = []
        for a in range(3):
            p0, p1, p2 = [
                jnp.dot(flat, weights[a, b, :, span], preferred_element_type=F32)
                for b in range(3)
            ]
            middle = p1[rows : rows + size]
            columns.append(
                (
                    p0[:size] + middle + p2[rows : rows + size],
                    p0[rows : rows + size] + middle + p2[2 * rows : 2 * rows + size],
                )
            )
        for lane in range(0, 256, 128):
            for dj in range(2):
                c0, c1, c2 = [columns[a][dj][:, lane : lane + 128] for a in range(3)]
                above = jnp.where(place == 0, 0.0, pltpu.roll(c0, 1, 0))
                below = jnp.where(place == rows - 1, 0.0, pltpu.roll(c2, size - 1, 0))
                for di, value in enumerate((above + c1 + c2, c0 + c1 + below)):
                    for j in range(width):
                        first = di * out_cols + 2 * j + dj
                        spread[pl.ds(first, rows, stride=2 * out_cols), :] = value[
                            j * rows : (j + 1) * rows
                        ]
            out[:, :, start + lane : start + lane + 128] = (
                spread[...].astype(BF16).reshape(2 * rows, out_cols, 128)
            )


def upsample(info, where, arrived, mine, theirs, ends, rows, width, per):
    channels = arrived.shape[2]
    framed, line = width + 2, arrived.shape[0] * GRID
    shapes = [(2 * rows, 2 * width, channels)]
    if arrived.shape[1] > rows:
        shapes.append((per, line, channels))
    return pl.pallas_call(
        upsample_kernel,
        out_shape=tuple(jax.ShapeDtypeStruct(shape, BF16) for shape in shapes),
        in_specs=[SMEM, SMEM, VMEM] + [ANY] * 6,
        out_specs=tuple(VMEM for _ in shapes),
        scratch_shapes=[
            pltpu.VMEM((line, 128), F32),
            pltpu.VMEM((framed, rows, channels), BF16),
            pltpu.VMEM((3, 3, channels, channels), BF16),
            pltpu.VMEM((4 * rows * width, 128), F32),
            pltpu.SemaphoreType.DMA((8,)),
        ],
        compiler_params=params(40),
        cost_estimate=cost(18 * framed * rows * channels * channels, 18 * channels * channels),
        name="upsample",
    )(info, where, arrived, mine, theirs, *ends)


def settle_kernel(arrived, earlier, out, spread):
    per, _, channels = out.shape
    groups = arrived.shape[0]
    cells = out.shape[1] // groups
    for r in range(per):
        for lane in range(0, channels, 128):
            for c in range(groups):
                spread[pl.ds(c, cells, stride=groups), :] = arrived[
                    c, r * cells : (r + 1) * cells, lane : lane + 128
                ].astype(F32)
            out[r, :, lane : lane + 128] = spread[...].astype(BF16)


def settle(arrived, earlier, per):
    groups, cells, channels = arrived.shape[0], GRID, arrived.shape[2]
    return pl.pallas_call(
        settle_kernel,
        out_shape=jax.ShapeDtypeStruct((per, groups * cells, channels), BF16),
        in_specs=[VMEM, ANY],
        out_specs=VMEM,
        scratch_shapes=[pltpu.VMEM((groups * cells, 128), F32)],
        compiler_params=params(8),
        name="settle",
    )(arrived, earlier)


def on_device(
    latent, conv_first, conv_second, w_query, w_key, w_value, w_out, w_in, w_down, conv_up
):
    n = lax.axis_size("row")
    chips = n // 2
    device = lax.axis_index("row")
    core, chip = device % 2, device // 2
    per, cols, channels = latent.shape
    half = channels // 2
    flip = lax.axis_index("parts") % 2 == 1
    swap = [(i, i ^ 1) for i in range(n)]

    def unit_of(share):
        mine = lax.dynamic_slice_in_dim(share, core * half, half, axis=share.ndim - 1)
        given = lax.dynamic_slice_in_dim(share, (1 - core) * half, half, axis=share.ndim - 1)
        got = lax.ppermute(given, "row", swap)
        depth = share.ndim - 2
        return jnp.where(
            core == 0,
            jnp.concatenate([mine, got], axis=depth),
            jnp.concatenate([got, mine], axis=depth),
        )

    units = unit_of(jnp.stack([conv_first, conv_second, conv_up], axis=1))
    pair, last = Gather(units[:, :2], flip, False), Gather(units[:, 2:], flip, True)
    count = chips // 2
    pair.step(1)
    latent_later, _ = lax.optimization_barrier((latent, pair.up))

    edges = []
    for i in range(chips - 1):
        edges += [(2 * i + 1, 2 * i + 2), (2 * i + 2, 2 * i + 1)]
    beside = jnp.where(core == 0, latent_later[:2], latent_later[-2:])
    near = lax.ppermute(beside, "row", edges)
    partner = lax.ppermute(latent_later, "row", swap)
    far = lax.ppermute(near, "row", swap)
    for index in range(2, count):
        if len(pair.batches) > 1:
            pair.after(pair.batches[-2])
        pair.step(index)
    since, joint = pair.sent, list(pair.batches)
    pair.cross(slice(0, 1))
    last.after(pair.up)
    last.step(1)
    pair.after((joint[-1], near, partner))
    pair.step(count)
    pair.finals = last.before(pair.finals)
    pair.cross_final(0)
    field = jnp.where(
        core == 0,
        jnp.concatenate([near, latent, partner, far], axis=0),
        jnp.concatenate([far, partner, latent, near], axis=0),
    )
    active = gelu(field.astype(F32)).astype(BF16)
    active, pair.finals[1] = lax.optimization_barrier((active, pair.finals[1]))
    first_pieces = pair.result()
    pair.batches = joint + [pair.cross_late(1, since)]
    last.after(active)
    last.step(2)

    place = jnp.where(chip % 2 == 0, chip // 2, chips - 1 - chip // 2)
    owners = chip_at((place + jnp.array(ring_positions(chips), jnp.int32)) % chips, chips)
    top = jnp.where(chip == 0, 1, 0)
    bottom = 2 * per + 2 - jnp.where(chip == chips - 1, 1, 0)
    where = jnp.concatenate(
        [jnp.where(flip, 2, 0)[None], owners, jnp.stack([core, top, bottom])]
    ).astype(jnp.int32)

    y1, active2 = first_conv(where, active, field, first_pieces, 3)
    active2 = last.before(active2)
    active2, pair.batches = lax.optimization_barrier((active2, pair.batches))
    second_pieces = pair.result()
    theirs = lax.ppermute(active2, "row", swap)
    last.after(active2)
    for index in range(3, count):
        last.step(index)
    y2 = second_conv(where, y1, active2, theirs, second_pieces, 4)

    y2 = last.before(y2)
    groups = cols // GRID
    subs = n // groups
    index_groups = None
    if subs > 1:
        index_groups = [[k * subs + s for k in range(groups)] for s in range(subs)]
    if subs > 1:
        kept = lax.dynamic_slice_in_dim(y2, core * per, per, axis=1)
        passed = lax.dynamic_slice_in_dim(y2, (1 - core) * per, per, axis=1)
        partner = lax.ppermute(passed, "row", swap)
        y2 = jnp.where(
            core == 0,
            jnp.concatenate([kept, partner], axis=3),
            jnp.concatenate([partner, kept], axis=3),
        )
    owned = lax.all_to_all(
        y2, "row", split_axis=0, concat_axis=0, axis_index_groups=index_groups, tiled=True
    )
    up_mine = assemble(where, last.result(), chips)
    owned, _ = lax.optimization_barrier((owned, up_mine))
    up_theirs = lax.ppermute(up_mine, "row", swap)
    last.after(owned)
    last.step(count)
    sides = 2 if subs == 1 else 1
    owned = owned.reshape(GRID // 2, sides, 2, per, GRID, channels // sides)
    width = cols // 2 // n
    dests = jnp.arange(n, dtype=jnp.int32)
    starts = cols // 4 + width * dests - 1
    column = device // subs
    picks = jnp.clip((starts - column + groups - 1) // groups, 0, GRID - 1).astype(jnp.int32)
    sent = windows(subs == 1, picks, owned, w_query, w_key, w_value, w_out, w_in, w_down)

    sent = last.before(sent)
    sent, last.finals = lax.optimization_barrier((sent, last.finals))
    last.cross_final(0)
    back = lax.all_to_all(
        sent[0],
        "row",
        split_axis=0,
        concat_axis=0,
        axis_index_groups=index_groups,
        tiled=True,
    )
    central = back
    rows = subs * per * GRID // 2
    if subs > 1:
        central = lax.all_to_all(sent[1], "row", split_axis=0, concat_axis=0, tiled=True)
        central = central.reshape(groups, subs, GRID // 2, per, channels)
        central = central.transpose(0, 2, 1, 3, 4).reshape(groups, rows, channels)
    ends = [last.finals[0], last.batches[-1]]
    ends += [lax.ppermute(end, "row", swap) for end in ends]
    sources = (cols // 4 + width * device - 1 + jnp.arange(width + 2, dtype=jnp.int32)) % groups
    info = jnp.concatenate(
        [jnp.stack([core, (device > 0).astype(jnp.int32), (device < n - 1).astype(jnp.int32)]), sources]
    ).astype(jnp.int32)
    upsampled, *settled = upsample(
        info, where, central, up_mine, up_theirs, ends, rows, width, per
    )
    latent_out = settled[0] if settled else settle(back, upsampled, per)
    return (latent_out, upsampled)


def solution(mesh):
    placed = (
        P(("parts", "row"), None, None),
        P(None, None, "row", None),
        P(None, None, "row", None),
        P(),
        P(),
        P(),
        P(),
        P(),
        P(),
        P(None, None, "row", None),
    )
    return jax.shard_map(
        on_device,
        mesh=mesh,
        in_specs=placed,
        out_specs=(P(("parts", "row"), None, None), P("parts", "row", None)),
        check_vma=False,
    )
```

```python
import functools

import jax
import jax.numpy as jnp
from jax import lax
from jax.experimental import pallas as pl
from jax.experimental.pallas import tpu as pltpu
from jax.sharding import PartitionSpec as P

HD = 64
GRID = 16
F32, BF16 = jnp.float32, jnp.bfloat16
ANY = pl.BlockSpec(memory_space=pl.ANY)
VMEM = pl.BlockSpec(memory_space=pltpu.VMEM)
SMEM = pl.BlockSpec(memory_space=pltpu.SMEM)


def gelu(x):
    return jax.nn.gelu(x, approximate=True)


def params(mib):
    return pltpu.CompilerParams(vmem_limit_bytes=mib << 20)


def cost(flops, size, transcendentals=0):
    return pl.CostEstimate(
        flops=int(flops), bytes_accessed=int(size), transcendentals=int(transcendentals)
    )


def chip_at(position, chips):
    return jnp.where(position < chips // 2, 2 * position, 2 * (chips - 1 - position) + 1)


def ring_of(chips):
    return list(range(0, chips, 2)) + list(range(1, chips, 2))[::-1]


def ring_positions(chips):
    steps = [0]
    for step in range(1, chips // 2 + 1):
        steps.append(-step)
        if step <= (chips - 1) // 2:
            steps.append(step)
    return steps


class Gather:
    def __init__(self, unit, flip, whole):
        turned = jnp.where(flip, unit[::-1], unit)
        self.chips, self.whole = lax.axis_size("row") // 2, whole
        self.up = self.down = turned[:2]
        self.rest = turned[2]
        self.pieces, self.finals, self.batches, self.sent = [self.up], [], [], 1

    def after(self, value):
        self.up, self.down, _ = lax.optimization_barrier((self.up, self.down, value))

    def before(self, value):
        held = (value, self.up, self.down, self.finals, self.batches[:-1])
        return lax.optimization_barrier(held)[0]

    def step(self, index):
        ring = ring_of(self.chips)
        forward = [
            (2 * ring[i] + core, 2 * ring[(i + 1) % self.chips] + core)
            for i in range(self.chips)
            for core in (0, 1)
        ]
        backward = [(b, a) for a, b in forward]
        across = [(i, i ^ 1) for i in range(lax.axis_size("parts"))]
        if index == self.chips // 2:
            ways = ((self.up, forward), (self.down, backward))
            for kernel in range(self.up.shape[1]):
                value, pairs = ways[kernel % 2]
                self.finals.append(lax.ppermute(value[:, kernel : kernel + 1], "row", pairs))
            return
        self.up = lax.ppermute(self.up, "row", forward)
        self.down = lax.ppermute(self.down, "row", backward)
        self.pieces += [self.up, self.down]
        near = len(self.pieces) < self.chips - 1
        if (near and len(self.pieces) - self.sent >= self.chips // 4) or (not near and self.whole):
            self.cross(slice(None))

    def cross(self, kernels):
        across = [(i, i ^ 1) for i in range(lax.axis_size("parts"))]
        thirds = [piece[0, kernels] for piece in self.pieces[self.sent :]]
        self.batches.append(lax.ppermute(jnp.stack(thirds), "parts", across))
        self.sent = len(self.pieces)

    def cross_final(self, kernel):
        across = [(i, i ^ 1) for i in range(lax.axis_size("parts"))]
        self.batches.append(lax.ppermute(self.finals[kernel][:1], "parts", across))

    def cross_late(self, kernel, since):
        across = [(i, i ^ 1) for i in range(lax.axis_size("parts"))]
        late = self.pieces[since:] + self.finals[kernel : kernel + 1]
        thirds = [piece[0, -1:] for piece in late]
        return lax.ppermute(jnp.stack(thirds), "parts", across)

    def result(self):
        return self.pieces + self.finals + [self.rest] + self.batches


def start_copies(where, refs, index, target, sems, final=True):
    chips = target.shape[2] // refs[0].shape[3]
    near, kernels = chips - 1, refs[0].shape[1] if final else 0
    finals, rest = refs[near : near + kernels], refs[near + kernels]
    batches = refs[near + kernels + 1 :]
    pieces = [piece.at[:, index] for piece in refs[:near]]
    pieces += [piece.at[:, 0] for piece in finals[index : index + 1]]
    thirds = [rest.at[index]]
    for batch in batches:
        kernel = min(index, batch.shape[1] - 1)
        thirds += [batch.at[i, kernel] for i in range(batch.shape[0])]
    first = where[0]
    share = refs[0].shape[3]
    jobs = []
    for i, piece in enumerate(pieces):
        rows = pl.ds(pl.multiple_of(where[1 + i] * share, share), share)
        jobs.append((piece.at[0], target.at[first, :, rows, :]))
        jobs.append((piece.at[1], target.at[1, :, rows, :]))
        jobs.append((thirds[i], target.at[2 - first, :, rows, :]))
    copies = [
        pltpu.make_async_copy(source, dest, sems.at[i]) for i, (source, dest) in enumerate(jobs)
    ]
    for copy in copies:
        copy.start()
    return copies


def assemble_kernel(where, *refs):
    target, sems = refs[-2:]
    for copy in start_copies(where, refs[:-2], 0, target, sems, False):
        copy.wait()


def assemble(where, pieces, chips):
    share, outs = pieces[0].shape[3:]
    shape = (3, 3, share * chips, outs)
    return pl.pallas_call(
        assemble_kernel,
        out_shape=jax.ShapeDtypeStruct(shape, BF16),
        in_specs=[SMEM] + [ANY] * len(pieces),
        out_specs=VMEM,
        scratch_shapes=[pltpu.SemaphoreType.DMA((3 * chips,))],
        compiler_params=params(12),
        cost_estimate=cost(0, 4 * 9 * share * chips * outs),
        name="assemble",
    )(where, *pieces)


def conv_rows(lefts, weights, depths, row, rows, cols):
    total = []
    for b in range(3):
        part = None
        for a in range(3):
            for left, depth in zip(lefts, depths):
                block = left(row + a, rows).reshape(rows * cols, -1)
                term = jnp.dot(block, weights[a, b, depth, :], preferred_element_type=F32)
                part = term if part is None else part + term
        total.append(part)
    size = rows * cols
    col = lax.broadcasted_iota(jnp.int32, total[0].shape, 0) % cols
    left = jnp.where(col == 0, 0.0, pltpu.roll(total[0], 1, 0))
    right = jnp.where(col == cols - 1, 0.0, pltpu.roll(total[2], size - 1, 0))
    return left + total[1] + right


def first_conv_kernel(step, where, act, lat, *refs):
    pieces, (y_out, act_out, weights, sems) = refs[:-4], refs[-4:]
    copies = start_copies(where, pieces, 0, weights, sems)
    core, top, bottom = where[where.shape[0] - 3], where[where.shape[0] - 2], where[where.shape[0] - 1]
    rows, cols, half = y_out.shape
    lanes = pl.ds(pl.multiple_of(core * half, half), half)
    for copy in copies:
        copy.wait()

    def body(i, carry):
        row = i * step
        mixed = conv_rows(
            [lambda r, k: act[pl.ds(r, k)]], weights, [slice(None)], row, step, cols
        ).reshape(step, cols, half)
        y = (lat[pl.ds(row + 1, step), :, lanes].astype(F32) + mixed).astype(BF16)
        y_out[pl.ds(row, step)] = y
        active = gelu(y.astype(F32))
        place = row + lax.broadcasted_iota(jnp.int32, active.shape, 0)
        active = jnp.where((place >= top) & (place < bottom), active, 0.0)
        act_out[pl.ds(row, step)] = active.astype(BF16)
        return carry

    lax.fori_loop(0, rows // step, body, 0)


def first_conv(where, act, lat, pieces, step):
    total_rows, cols, channels = act.shape
    rows, half, chips = total_rows - 2, channels // 2, channels // pieces[0].shape[3]
    out = jax.ShapeDtypeStruct((rows, cols, half), BF16)
    return pl.pallas_call(
        functools.partial(first_conv_kernel, step),
        out_shape=(out, out),
        in_specs=[SMEM, VMEM, VMEM] + [ANY] * len(pieces),
        out_specs=(VMEM, VMEM),
        scratch_shapes=[
            pltpu.VMEM((3, 3, channels, half), BF16),
            pltpu.SemaphoreType.DMA((3 * chips,)),
        ],
        compiler_params=params(40),
        cost_estimate=cost(
            18 * rows * cols * channels * half, 18 * channels * half, rows * cols * half
        ),
        name="first_conv",
    )(where, act, lat, *pieces)


def second_conv_kernel(step, where, y1, mine, theirs, *refs):
    pieces, (send, weights, sems, spread) = refs[:-4], refs[-4:]
    copies = start_copies(where, pieces, 1, weights, sems)
    core = where[where.shape[0] - 3]
    groups, rows, _, half = send.shape
    cols = mine.shape[1]
    own = pl.ds(pl.multiple_of(core * half, half), half)
    other = pl.ds(pl.multiple_of((1 - core) * half, half), half)
    for copy in copies:
        copy.wait()
    lefts = [lambda r, k: mine[pl.ds(r, k)], lambda r, k: theirs[pl.ds(r, k)]]
    for row in range(0, rows, step):
        mixed = conv_rows(lefts, weights, [own, other], row, step, cols)
        before = y1[pl.ds(row + 1, step)].reshape(step * cols, half).astype(F32)
        rounded = (before + mixed).astype(BF16).astype(F32)
        for lane in range(0, half, 128):
            spread[...] = rounded[:, lane : lane + 128]
            for r in range(step):
                for c in range(groups):
                    send[c, row + r, :, lane : lane + 128] = spread[
                        pl.ds(r * cols + c, cols // groups, stride=groups), :
                    ].astype(BF16)


def second_conv(where, y1, mine, theirs, pieces, step):
    padded_rows, cols, half = y1.shape
    rows, channels = padded_rows - 2, 2 * half
    groups, chips = cols // GRID, channels // pieces[0].shape[3]
    return pl.pallas_call(
        functools.partial(second_conv_kernel, step),
        out_shape=jax.ShapeDtypeStruct((groups, rows, GRID, half), BF16),
        in_specs=[SMEM, VMEM, VMEM, VMEM] + [ANY] * len(pieces),
        out_specs=VMEM,
        scratch_shapes=[
            pltpu.VMEM((3, 3, channels, half), BF16),
            pltpu.SemaphoreType.DMA((3 * chips,)),
            pltpu.VMEM((step * cols, 128), F32),
        ],
        compiler_params=params(40),
        cost_estimate=cost(18 * rows * cols * channels * half, 18 * channels * half),
        name="second_conv",
    )(where, y1, mine, theirs, *pieces)


def rms_round(values):
    meansq = jnp.mean(values * values, axis=-1, keepdims=True)
    return (values * lax.rsqrt(meansq + 1e-06)).astype(BF16)


def window_kernel(per, picks, y2, *refs):
    sources, outs, sems = refs[:6], refs[6:-10], refs[-1]
    (att, wide, thin), weights = refs[-10:-7], refs[-7:-1]
    out, edge = outs[0], outs[-1]
    copies = [
        pltpu.make_async_copy(source, dest, sems.at[i])
        for i, (source, dest) in enumerate(zip(sources, weights))
    ]
    for copy in copies:
        copy.start()
    w_query, w_key, w_value, w_out, w_in, w_down = weights
    grid, channels = out.shape[0], out.shape[2]
    cells = grid * GRID
    current = jnp.concatenate(
        [
            jnp.concatenate(
                [y2[:, side, :, r].reshape(cells, -1) for side in range(y2.shape[1])], axis=1
            )
            for r in range(per)
        ],
        axis=0,
    ).astype(F32)
    normed = rms_round(current)
    dot = functools.partial(jnp.dot, preferred_element_type=F32)
    for copy in copies[:3]:
        copy.wait()
    queries = (dot(normed, w_query[...]).astype(BF16) * BF16(HD**-0.5)).astype(BF16)
    keys = dot(normed, w_key[...]).astype(BF16)
    values = dot(normed, w_value[...]).astype(BF16)
    pair = 2 * HD
    low = lax.broadcasted_iota(jnp.int32, (cells, pair), 1) < HD
    zero = jnp.zeros((cells, pair), BF16)
    for r in range(per):
        for lane in range(0, channels, pair):
            spot = (slice(r * cells, (r + 1) * cells), slice(lane, lane + pair))
            query, key, value = queries[spot], keys[spot], values[spot]
            halves = []
            for keep in (jnp.where(low, query, zero), jnp.where(low, zero, query)):
                scores = lax.dot_general(
                    keep, key, (((1,), (1,)), ((), ())), preferred_element_type=F32
                )
                lifted = jnp.exp(scores - jnp.max(scores, axis=-1, keepdims=True))
                share = 1.0 / jnp.sum(lifted, axis=-1, keepdims=True)
                halves.append(dot(lifted.astype(BF16), value) * share)
            att[spot] = jnp.where(low, halves[0], halves[1]).astype(BF16)
    copies[3].wait()
    current = (current + dot(att[...], w_out[...])).astype(BF16).astype(F32)
    normed = rms_round(current)
    units = w_in.shape[1]
    chunk = units // 2
    lowered = None
    for copy in copies[4:]:
        copy.wait()
    for start in range(0, units, chunk):
        span = slice(start, start + chunk)
        hidden = gelu(dot(normed, w_in[:, span])).astype(BF16)
        term = dot(hidden, w_down[span, :])
        lowered = term if lowered is None else lowered + term
    latent = (current + lowered).astype(BF16)
    wide_values = latent.astype(F32)
    for r in range(per):
        out[:, r * GRID : (r + 1) * GRID] = latent[r * cells : (r + 1) * cells].reshape(
            grid, GRID, channels
        )
    kept = grid // 2
    for lane in range(0, channels, 128):
        wide[...] = wide_values[:, lane : lane + 128]
        for d in range(picks.shape[0]):
            for r in range(per):
                first = r * cells + (grid // 4) * GRID + picks[d]
                thin[pl.ds(d * kept * per + r, kept, stride=per), :] = wide[
                    pl.ds(first, kept, stride=GRID), :
                ]
        edge[:, edge.shape[1] - kept * per :, lane : lane + 128] = (
            thin[...].astype(BF16).reshape(picks.shape[0], kept * per, 128)
        )


def windows(joined, picks, y2, w_query, w_key, w_value, w_out, w_in, w_down):
    grid, per, channels = y2.shape[0] * y2.shape[2], y2.shape[3], w_query.shape[0]
    cells, units, dests = grid * GRID, w_in.shape[1], picks.shape[0]
    total = per * cells
    kept = per * grid // 2
    flops = 2 * total * channels * (4 * channels + 2 * units + 2 * cells)
    shapes = [(grid, per * GRID, channels), (dests, kept, channels)]
    if joined:
        shapes = [(grid, per * GRID + kept, channels)]
    return pl.pallas_call(
        functools.partial(window_kernel, per),
        out_shape=tuple(jax.ShapeDtypeStruct(shape, BF16) for shape in shapes),
        in_specs=[SMEM, VMEM] + [ANY] * 6,
        out_specs=tuple(VMEM for _ in shapes),
        scratch_shapes=[
            pltpu.VMEM((total, channels), BF16),
            pltpu.VMEM((total, 128), F32),
            pltpu.VMEM((dests * kept, 128), F32),
        ]
        + [
            pltpu.VMEM(weight.shape, BF16)
            for weight in (w_query, w_key, w_value, w_out, w_in, w_down)
        ]
        + [pltpu.SemaphoreType.DMA((6,))],
        compiler_params=params(56),
        cost_estimate=cost(flops, 8 * total * channels, total * (cells * 8 + units)),
        name="windows",
    )(picks, y2, w_query, w_key, w_value, w_out, w_in, w_down)


def upsample_kernel(info, where, arrived, mine, theirs, *refs):
    ends, outs, (lines, field, weights, spread, sems) = refs[:4], refs[4:-5], refs[-5:]
    out = outs[0]
    taps, depth, half = mine.shape[0], mine.shape[2], mine.shape[3]
    core = info[0]
    copies = []
    for index, (source, side) in enumerate(((mine, core), (theirs, 1 - core))):
        lanes = pl.ds(pl.multiple_of(side * half, half), half)
        copies.append(pltpu.make_async_copy(source, weights.at[:, :, :, lanes], sems.at[index]))
    for copy in copies:
        copy.start()
    framed, rows, channels = field.shape
    width = framed - 2
    for settled in outs[1:]:
        settle_kernel(arrived, None, settled, lines)
    for j in range(framed):
        column = arrived[info[3 + j], pl.ds(arrived.shape[1] - rows, rows)]
        if j == 0:
            column = column * info[1].astype(F32).astype(BF16)
        if j == framed - 1:
            column = column * info[2].astype(F32).astype(BF16)
        field[j] = column
    for copy in copies:
        copy.wait()
    share = ends[0].shape[3]
    far = where[where.shape[0] - 4]
    depth_rows = pl.ds(pl.multiple_of(far * share, share), share)
    late = []
    for side, (pair, third) in ((core, ends[:2]), (1 - core, ends[2:])):
        lanes = pl.ds(pl.multiple_of(side * half, half), half)
        for source, tap in ((pair.at[0, 0], where[0]), (pair.at[1, 0], 1), (third.at[0, 0], 2 - where[0])):
            target = weights.at[tap, :, depth_rows, lanes]
            late.append(pltpu.make_async_copy(source, target, sems.at[2 + len(late)]))
    for copy in late:
        copy.start()
    for copy in late:
        copy.wait()
    flat = field[...].reshape(framed * rows, channels)
    size = width * rows
    place = lax.broadcasted_iota(jnp.int32, (size, 128), 0) % rows
    out_cols = 2 * width
    for start in range(0, channels, 256):
        span = slice(start, start + 256)
        columns = []
        for a in range(3):
            p0, p1, p2 = [
                jnp.dot(flat, weights[a, b, :, span], preferred_element_type=F32)
                for b in range(3)
            ]
            middle = p1[rows : rows + size]
            columns.append(
                (
                    p0[:size] + middle + p2[rows : rows + size],
                    p0[rows : rows + size] + middle + p2[2 * rows : 2 * rows + size],
                )
            )
        for lane in range(0, 256, 128):
            for dj in range(2):
                c0, c1, c2 = [columns[a][dj][:, lane : lane + 128] for a in range(3)]
                above = jnp.where(place == 0, 0.0, pltpu.roll(c0, 1, 0))
                below = jnp.where(place == rows - 1, 0.0, pltpu.roll(c2, size - 1, 0))
                for di, value in enumerate((above + c1 + c2, c0 + c1 + below)):
                    for j in range(width):
                        first = di * out_cols + 2 * j + dj
                        spread[pl.ds(first, rows, stride=2 * out_cols), :] = value[
                            j * rows : (j + 1) * rows
                        ]
            out[:, :, start + lane : start + lane + 128] = (
                spread[...].astype(BF16).reshape(2 * rows, out_cols, 128)
            )


def upsample(info, where, arrived, mine, theirs, ends, rows, width, per):
    channels = arrived.shape[2]
    framed, line = width + 2, arrived.shape[0] * GRID
    shapes = [(2 * rows, 2 * width, channels)]
    if arrived.shape[1] > rows:
        shapes.append((per, line, channels))
    return pl.pallas_call(
        upsample_kernel,
        out_shape=tuple(jax.ShapeDtypeStruct(shape, BF16) for shape in shapes),
        in_specs=[SMEM, SMEM, VMEM] + [ANY] * 6,
        out_specs=tuple(VMEM for _ in shapes),
        scratch_shapes=[
            pltpu.VMEM((line, 128), F32),
            pltpu.VMEM((framed, rows, channels), BF16),
            pltpu.VMEM((3, 3, channels, channels), BF16),
            pltpu.VMEM((4 * rows * width, 128), F32),
            pltpu.SemaphoreType.DMA((8,)),
        ],
        compiler_params=params(40),
        cost_estimate=cost(18 * framed * rows * channels * channels, 18 * channels * channels),
        name="upsample",
    )(info, where, arrived, mine, theirs, *ends)


def settle_kernel(arrived, earlier, out, spread):
    per, _, channels = out.shape
    groups = arrived.shape[0]
    cells = out.shape[1] // groups
    for r in range(per):
        for lane in range(0, channels, 128):
            for c in range(groups):
                spread[pl.ds(c, cells, stride=groups), :] = arrived[
                    c, r * cells : (r + 1) * cells, lane : lane + 128
                ].astype(F32)
            out[r, :, lane : lane + 128] = spread[...].astype(BF16)


def settle(arrived, earlier, per):
    groups, cells, channels = arrived.shape[0], GRID, arrived.shape[2]
    return pl.pallas_call(
        settle_kernel,
        out_shape=jax.ShapeDtypeStruct((per, groups * cells, channels), BF16),
        in_specs=[VMEM, ANY],
        out_specs=VMEM,
        scratch_shapes=[pltpu.VMEM((groups * cells, 128), F32)],
        compiler_params=params(8),
        name="settle",
    )(arrived, earlier)


def on_device(
    latent, conv_first, conv_second, w_query, w_key, w_value, w_out, w_in, w_down, conv_up
):
    n = lax.axis_size("row")
    chips = n // 2
    device = lax.axis_index("row")
    core, chip = device % 2, device // 2
    per, cols, channels = latent.shape
    half = channels // 2
    flip = lax.axis_index("parts") % 2 == 1
    swap = [(i, i ^ 1) for i in range(n)]

    def unit_of(share):
        mine = lax.dynamic_slice_in_dim(share, core * half, half, axis=share.ndim - 1)
        given = lax.dynamic_slice_in_dim(share, (1 - core) * half, half, axis=share.ndim - 1)
        got = lax.ppermute(given, "row", swap)
        depth = share.ndim - 2
        return jnp.where(
            core == 0,
            jnp.concatenate([mine, got], axis=depth),
            jnp.concatenate([got, mine], axis=depth),
        )

    units = unit_of(jnp.stack([conv_first, conv_second, conv_up], axis=1))
    pair, last = Gather(units[:, :2], flip, False), Gather(units[:, 2:], flip, True)
    count = chips // 2
    pair.step(1)
    latent_later, _ = lax.optimization_barrier((latent, pair.up))

    edges = []
    for i in range(chips - 1):
        edges += [(2 * i + 1, 2 * i + 2), (2 * i + 2, 2 * i + 1)]
    beside = jnp.where(core == 0, latent_later[:2], latent_later[-2:])
    near = lax.ppermute(beside, "row", edges)
    partner = lax.ppermute(latent_later, "row", swap)
    far = lax.ppermute(near, "row", swap)
    for index in range(2, count):
        if len(pair.batches) > 1:
            pair.after(pair.batches[-2])
        pair.step(index)
    since, joint = pair.sent, list(pair.batches)
    pair.cross(slice(0, 1))
    last.after(pair.up)
    last.step(1)
    pair.after((joint[-1], near, partner))
    pair.step(count)
    pair.finals = last.before(pair.finals)
    pair.cross_final(0)
    field = jnp.where(
        core == 0,
        jnp.concatenate([near, latent, partner, far], axis=0),
        jnp.concatenate([far, partner, latent, near], axis=0),
    )
    active = gelu(field.astype(F32)).astype(BF16)
    active, pair.finals[1] = lax.optimization_barrier((active, pair.finals[1]))
    first_pieces = pair.result()
    pair.batches = joint + [pair.cross_late(1, since)]
    last.after(active)
    last.step(2)

    place = jnp.where(chip % 2 == 0, chip // 2, chips - 1 - chip // 2)
    owners = chip_at((place + jnp.array(ring_positions(chips), jnp.int32)) % chips, chips)
    top = jnp.where(chip == 0, 1, 0)
    bottom = 2 * per + 2 - jnp.where(chip == chips - 1, 1, 0)
    where = jnp.concatenate(
        [jnp.where(flip, 2, 0)[None], owners, jnp.stack([core, top, bottom])]
    ).astype(jnp.int32)

    y1, active2 = first_conv(where, active, field, first_pieces, 3)
    active2 = last.before(active2)
    active2, pair.batches = lax.optimization_barrier((active2, pair.batches))
    second_pieces = pair.result()
    theirs = lax.ppermute(active2, "row", swap)
    last.after(active2)
    for index in range(3, count):
        last.step(index)
    y2 = second_conv(where, y1, active2, theirs, second_pieces, 4)

    y2 = last.before(y2)
    groups = cols // GRID
    subs = n // groups
    index_groups = None
    if subs > 1:
        index_groups = [[k * subs + s for k in range(groups)] for s in range(subs)]
    if subs > 1:
        kept = lax.dynamic_slice_in_dim(y2, core * per, per, axis=1)
        passed = lax.dynamic_slice_in_dim(y2, (1 - core) * per, per, axis=1)
        partner = lax.ppermute(passed, "row", swap)
        y2 = jnp.where(
            core == 0,
            jnp.concatenate([kept, partner], axis=3),
            jnp.concatenate([partner, kept], axis=3),
        )
    owned = lax.all_to_all(
        y2, "row", split_axis=0, concat_axis=0, axis_index_groups=index_groups, tiled=True
    )
    up_mine = assemble(where, last.result(), chips)
    owned, _ = lax.optimization_barrier((owned, up_mine))
    up_theirs = lax.ppermute(up_mine, "row", swap)
    last.after(owned)
    last.step(count)
    sides = 2 if subs == 1 else 1
    owned = owned.reshape(GRID // 2, sides, 2, per, GRID, channels // sides)
    width = cols // 2 // n
    dests = jnp.arange(n, dtype=jnp.int32)
    starts = cols // 4 + width * dests - 1
    column = device // subs
    picks = jnp.clip((starts - column + groups - 1) // groups, 0, GRID - 1).astype(jnp.int32)
    sent = windows(subs == 1, picks, owned, w_query, w_key, w_value, w_out, w_in, w_down)

    sent = last.before(sent)
    sent, last.finals = lax.optimization_barrier((sent, last.finals))
    last.cross_final(0)
    back = lax.all_to_all(
        sent[0],
        "row",
        split_axis=0,
        concat_axis=0,
        axis_index_groups=index_groups,
        tiled=True,
    )
    central = back
    rows = subs * per * GRID // 2
    if subs > 1:
        central = lax.all_to_all(sent[1], "row", split_axis=0, concat_axis=0, tiled=True)
        central = central.reshape(groups, subs, GRID // 2, per, channels)
        central = central.transpose(0, 2, 1, 3, 4).reshape(groups, rows, channels)
    ends = [last.finals[0], last.batches[-1]]
    ends += [lax.ppermute(end, "row", swap) for end in ends]
    sources = (cols // 4 + width * device - 1 + jnp.arange(width + 2, dtype=jnp.int32)) % groups
    info = jnp.concatenate(
        [jnp.stack([core, (device > 0).astype(jnp.int32), (device < n - 1).astype(jnp.int32)]), sources]
    ).astype(jnp.int32)
    upsampled, *settled = upsample(
        info, where, central, up_mine, up_theirs, ends, rows, width, per
    )
    latent_out = settled[0] if settled else settle(back, upsampled, per)
    return (latent_out, upsampled)


def solution(mesh):
    placed = (
        P(("parts", "row"), None, None),
        P(None, None, "row", None),
        P(None, None, "row", None),
        P(),
        P(),
        P(),
        P(),
        P(),
        P(),
        P(None, None, "row", None),
    )
    return jax.shard_map(
        on_device,
        mesh=mesh,
        in_specs=placed,
        out_specs=(P(("parts", "row"), None, None), P("parts", "row", None)),
        check_vma=False,
    )
```
